32 devices in a mesh: normal: 4 (over z), span: 2 (over x), stream: 4 (over y, core).
Axes of the slice: x: 2, y: 2, z: 4, core: 2. Of those that a mesh axis runs over, the one named last changes fastest.
Arguments:
- iterate: float32 [192, 5, 2, 512], P('normal', None, 'span', 'stream'), may hold values from -6 to 6
- source: float32 [192, 5, 2, 512], P('normal', None, 'span', 'stream'), may hold values from -6 to 6
- pivot: float32 [192, 5, 5, 2, 512], P('normal', None, None, 'span', 'stream'), as said below
- lower: float32 [192, 5, 5, 2, 512], P('normal', None, None, 'span', 'stream'), as said below
- upper: float32 [192, 5, 5, 2, 512], P('normal', None, None, 'span', 'stream'), as said below
- coupling: float32 [4, 192, 5, 5, 2, 512], P(None, 'normal', None, None, 'span', 'stream'), may hold values from -0.6 to 0.6
- iblank: int32 [192, 2, 512], P('normal', 'span', 'stream'), may hold values from 0 to 2
- donor: int32 [192, 2, 512], P('normal', 'span', 'stream'), may hold values from 0 to 6143
Outputs:
- smoothed: float32 [192, 5, 2, 512], P('normal', None, 'span', 'stream')
The draws below stay inside these ranges and needn't reach their ends.
Inputs may be any that keep to these rules, and one draw needn't show every extreme that they name: `donor`: an offset within a tile of 48 x 1 x 128 points. pivot blocks are full 5x5 blocks. lower and upper factor blocks are full 5x5 blocks; the recurrences stay bounded. upper factor blocks are full 5x5 blocks.
All inputs are finite; a program needn't handle non-finite values.
Results may differ from the reference program's by a relative error of at most 0.00018.
Values sent between devices are 32-bit elements; how exact they have to be, the bound alone decides.
A program may use at most 64 MiB of HBM per device.

```python
import math
import jax
import jax.numpy as jnp
from jax import lax

CN = 48
SP = 1
ST = 128
COMP = 5
SWEEPS = 2
LINE_POINTS = 192
SPAN = 2
STREAM = 512


def factored_block_list(key, lower_rate, higher_rate, include_spike_events, diagonal_polarity):
    rate_draw_key, perturbation_key, spike_event_key, displacement_key = jax.random.split(key, 4)
    eye = jnp.eye(5, dtype=jnp.float32)[None, :, :, None, None]
    rate = jnp.exp(jax.random.uniform(rate_draw_key, (1, 5, 1, SPAN, STREAM), jnp.float32, math.log(lower_rate), math.log(higher_rate)))
    jitter = jax.random.uniform(perturbation_key, (LINE_POINTS, 5, 1, SPAN, STREAM), jnp.float32, 0.7, 1.4)
    retain_flags = jnp.exp(-rate * jitter)
    if include_spike_events:
        spike_event = jax.random.uniform(spike_event_key, (LINE_POINTS, 1, 1, 1, 1), jnp.float32) < 4.0 / LINE_POINTS
        retain_flags = jnp.where(spike_event, retain_flags * 0.6, retain_flags)
    off = 0.01 * jax.random.normal(displacement_key, (LINE_POINTS, 5, 5, SPAN, STREAM), jnp.float32)
    return diagonal_polarity * retain_flags * eye + off * (1.0 - eye)


def draw_pivot(key, part):
    key_diag, displacement_key = jax.random.split(jax.random.fold_in(key, 11))
    eye = jnp.eye(5, dtype=jnp.float32)[None, :, :, None, None]
    diag = jnp.exp(jax.random.uniform(key_diag, (LINE_POINTS, 5, 1, SPAN, STREAM), jnp.float32, math.log(0.004), math.log(0.02)))
    off = 0.002 * jax.random.normal(displacement_key, (LINE_POINTS, 5, 5, SPAN, STREAM), jnp.float32)
    return diag * eye + off * (1.0 - eye)


def draw_lower(key, part):
    return factored_block_list(jax.random.fold_in(key, 23), 0.3 / LINE_POINTS, 1.0 / 30.0, True, -1.0)


def draw_upper(key, part):
    return factored_block_list(jax.random.fold_in(key, 37), 0.3 / LINE_POINTS, 1.0 / 30.0, True, 1.0)


def touch_ends(array, own_key, low, largest):
    longest = array.shape.index(max(array.shape))
    spots = []
    for shift in (0, 1):
        where = [jax.random.randint(jax.random.fold_in(own_key, axis), (), 0, length) for axis, length in enumerate(array.shape)]
        where[longest] = (where[longest] + shift) % array.shape[longest]
        spots.append(tuple(where))
    return array.at[spots[0]].set(low).at[spots[1]].set(largest)


def block_scale(own_key, extent, shards, smallest, top_value):
    gain = 1.0
    for axis_at, shards_of in shards:
        heights = jax.random.uniform(jax.random.fold_in(jax.random.fold_in(own_key, 6), axis_at), (shards_of,), jnp.float32, smallest / len(shards), top_value / len(shards))
        gain = gain * jnp.repeat(jnp.exp(heights), extent[axis_at] // shards_of).reshape((-1,) + (1,) * (len(extent) - 1 - axis_at))
    return gain


def centred(own_key, extent, deviation, most, pieces=(), held_as=jnp.bfloat16):
    values = jax.random.normal(own_key, extent, jnp.float32) * deviation
    if len(pieces) > 0:
        values = block_scale(own_key, extent, pieces, -0.22, 0.18) * values
    return jnp.clip(values, min=-most, max=most).astype(held_as)


def setup_inputs(seed: int = 0) -> dict:
    keys = jax.random.split(jax.random.key(seed), 9)
    return {
        "iterate": centred(keys[0], (LINE_POINTS, COMP, SPAN, STREAM), 1.0, 6.0, ((0, 4), (2, 2), (3, 4)), jnp.float32),
        "source": centred(keys[1], (LINE_POINTS, COMP, SPAN, STREAM), 1.0, 6.0, ((0, 4), (2, 2), (3, 4)), jnp.float32),
        "pivot": draw_pivot(jax.random.fold_in(keys[8], 71), 0),
        "lower": draw_lower(jax.random.fold_in(keys[8], 71), 0),
        "upper": draw_upper(jax.random.fold_in(keys[8], 71), 0),
        "coupling": centred(keys[5], (4, LINE_POINTS, COMP, COMP, SPAN, STREAM), 0.1, 0.6, ((1, 4), (4, 2), (5, 4)), jnp.float32),
        "iblank": touch_ends(jax.random.randint(keys[6], (LINE_POINTS, SPAN, STREAM), 0, 3), jax.random.fold_in(keys[6], 1), 0, 2).astype(jnp.int32),
        "donor": touch_ends(jax.random.randint(keys[7], (LINE_POINTS, SPAN, STREAM), 0, CN * SP * ST), jax.random.fold_in(keys[7], 1), 0, (CN * SP * ST) - 1).astype(jnp.int32),
    }


def one_sweep(x, source, pivot, lower, upper, coupling, iblank, donor):
    near = [jnp.roll(x, 1, axis=2), jnp.roll(x, -1, axis=2), jnp.roll(x, 1, axis=3), jnp.roll(x, -1, axis=3)]
    couple = jnp.zeros_like(x)
    for direc in range(4):
        couple = couple + jnp.sum(coupling[direc] * near[direc][:, :, None], axis=1)
    line_pos = jnp.arange(LINE_POINTS, dtype=jnp.int32)[:, None, None]
    span_pos = jnp.arange(SPAN, dtype=jnp.int32)[None, :, None]
    strm_pos = jnp.arange(STREAM, dtype=jnp.int32)[None, None, :]
    line_idx = (line_pos // CN) * CN + donor // (SP * ST)
    span_idx = (span_pos // SP) * SP + (donor // ST) % SP
    strm_idx = (strm_pos // ST) * ST + donor % ST
    donated = jnp.transpose(x, (0, 2, 3, 1))[line_idx, span_idx, strm_idx]
    donated = jnp.transpose(donated, (0, 3, 1, 2))
    flag = iblank[:, None]
    rhs = jnp.where(flag == 0, 0.0, source - couple + jnp.where(flag == 2, donated, 0.0))
    scaled = jnp.sum(pivot * rhs[:, None], axis=2)

    def forward(state, inputs):
        term, block = inputs
        state = term - jnp.sum(block * state[None], axis=1)
        return state, state

    start = jnp.zeros((COMP, SPAN, STREAM), jnp.float32)
    _, ys = lax.scan(forward, start, (scaled, lower))

    def backward(state, inputs):
        term, block = inputs
        state = term - jnp.sum(block * state[None], axis=1)
        return state, state

    _, xs = lax.scan(backward, start, (ys, upper), reverse=True)
    return xs


def reference(iterate, source, pivot, lower, upper, coupling, iblank, donor):
    x = iterate
    for sweep in range(SWEEPS):
        x = one_sweep(x, source, pivot, lower, upper, coupling, iblank, donor)
    return x
```

```python
import functools
import jax
import jax.numpy as jnp
from jax import lax
from jax.experimental import pallas as pl
from jax.experimental.pallas import tpu as pltpu
from jax.sharding import PartitionSpec as P

SWEEPS = 2
N = 5
K = 8
LANES = 128
MESH = pl.DeviceIdType.MESH


def mat_vec(mat, vec):
    return [functools.reduce(jnp.add, [mat[c][e] * vec[e] for e in range(N)]) for c in range(N)]


def mat_mat(left, right):
    return [
        [functools.reduce(jnp.add, [left[c][e] * right[e][f] for e in range(N)]) for f in range(N)]
        for c in range(N)
    ]


def mat_map(function, *mats):
    return [[function(*(m[c][e] for m in mats)) for e in range(N)] for c in range(N)]


def vec_add(a, b):
    return [p + q for p, q in zip(a, b)]


def kernel(sizes, per_chunk, x_hbm, src_hbm, piv_hbm, low_hbm, upp_hbm, cpl_hbm, ibl_hbm, don_hbm, out_ref,
           xb, src, piv, low, upp, cpl, ibl, don, plane, edge_out, edge_in, vec_all, map_all,
           fw, gw, bw, scan_f, scan_b, excl, base, work, donated,
           load_sem, span_send, span_recv, edge_send, edge_recv, vec_send, vec_recv, map_send, map_recv):
    J = per_chunk
    n_normal, n_span, n_stream = sizes
    me, sp, st = lax.axis_index("normal"), lax.axis_index("span"), lax.axis_index("stream")
    span_targets = [lax.rem(sp + 1, n_span)] if n_span == 2 else [lax.rem(sp + 1, n_span), lax.rem(sp + n_span - 1, n_span)]
    stream_targets = [lax.rem(st + 1, n_stream)] if n_stream == 2 else [lax.rem(st + 1, n_stream), lax.rem(st + n_stream - 1, n_stream)]
    sides_span, sides_stream = len(span_targets), len(stream_targets)

    pairs = [(x_hbm, xb.at[0]), (low_hbm, low), (upp_hbm, upp), (don_hbm, don), (cpl_hbm, cpl),
             (src_hbm, src), (ibl_hbm, ibl), (piv_hbm, piv)]
    loads = [pltpu.make_async_copy(a, b, load_sem.at[i]) for i, (a, b) in enumerate(pairs)]
    for load in loads:
        load.start()
    ld_x, ld_low, ld_upp, ld_don, ld_cpl, ld_src, ld_ibl, ld_piv = loads

    barrier = pltpu.get_barrier_semaphore()
    for t in span_targets:
        pl.semaphore_signal(barrier, inc=1, device_id={"span": t}, device_id_type=MESH)
    for t in stream_targets:
        pl.semaphore_signal(barrier, inc=1, device_id={"stream": t}, device_id_type=MESH)
    for o in range(1, n_normal):
        pl.semaphore_signal(barrier, inc=1, device_id={"normal": lax.rem(me + o, n_normal)}, device_id_type=MESH)
    pl.semaphore_wait(barrier, sides_span + sides_stream + n_normal - 1)

    def span_copies(sweep, source):
        return [
            pltpu.make_async_remote_copy(
                src_ref=source, dst_ref=plane.at[sweep, i], send_sem=span_send.at[sweep, i],
                recv_sem=span_recv.at[sweep, i], device_id={"span": t}, device_id_type=MESH)
            for i, t in enumerate(span_targets)
        ]

    def edge_copies(sweep):
        return [
            pltpu.make_async_remote_copy(
                src_ref=edge_out.at[sweep], dst_ref=edge_in.at[sweep, i], send_sem=edge_send.at[sweep, i],
                recv_sem=edge_recv.at[sweep, i], device_id={"stream": t}, device_id_type=MESH)
            for i, t in enumerate(stream_targets)
        ]

    def normal_copies(ref, sends, recvs):
        out = []
        for o in range(1, n_normal):
            out.append(pltpu.make_async_remote_copy(
                src_ref=ref.at[me], dst_ref=ref.at[me], send_sem=sends.at[o - 1], recv_sem=recvs.at[o - 1],
                device_id={"normal": lax.rem(me + o, n_normal)}, device_id_type=MESH))
        return out

    def normal_arrivals(ref, sends, recvs):
        out = []
        for o in range(1, n_normal):
            came = lax.rem(me + n_normal - o, n_normal)
            out.append(pltpu.make_async_remote_copy(
                src_ref=ref.at[me], dst_ref=ref.at[came], send_sem=sends.at[o - 1], recv_sem=recvs.at[o - 1],
                device_id={"normal": lax.rem(me + o, n_normal)}, device_id_type=MESH))
        return out

    lane = lax.broadcasted_iota(jnp.int32, (K, LANES), 1)
    chunk = lax.broadcasted_iota(jnp.int32, (K, LANES), 0)

    def vec_rows(ref, j):
        return [ref[pl.ds(j * N + c, K, stride=J * N), :] for c in range(N)]

    def mat_rows(ref, j, first=0):
        return [[ref[pl.ds(first + j * N * N + c * N + e, K, stride=J * N * N), :] for e in range(N)] for c in range(N)]

    def get_mat(ref, *at):
        return [[ref[(*at, c, e)] for e in range(N)] for c in range(N)]

    def put_mat(ref, mat, *at):
        for c in range(N):
            for e in range(N):
                ref[(*at, c, e)] = mat[c][e]

    def send_edges(sweep):
        packed = jnp.zeros((K, LANES), jnp.float32)
        for j in range(J):
            rows = vec_rows(xb.at[sweep], j)
            for c in range(N):
                i = j * N + c
                packed = jnp.where(lane // 2 == i, pltpu.roll(rows[c], 2 * i + 1, 1), packed)
        edge_out[sweep] = packed
        copies = edge_copies(sweep)
        for copy in copies:
            copy.start()
        return copies

    span_now = span_copies(0, x_hbm)
    for copy in span_now:
        copy.start()
    ld_x.wait()
    edge_now = send_edges(0)
    pending = list(span_now) + list(edge_now)

    ld_low.wait()
    ld_upp.wait()

    first = mat_map(lambda a: -a, mat_rows(low, 0))
    put_mat(fw, first, 0)

    def fw_step(j, carry):
        carry = mat_mat(mat_map(lambda a: -a, mat_rows(low, j)), carry)
        put_mat(fw, carry, j)
        return carry

    last_f = lax.fori_loop(1, J, fw_step, first)
    start_b = mat_map(lambda a: -a, mat_rows(upp, J - 1))
    put_mat(bw, start_b, J - 1)
    put_mat(gw, last_f, J - 1)

    def bw_step(i, carry):
        j = J - 2 - i
        carry = mat_mat(mat_map(lambda a: -a, mat_rows(upp, j)), carry)
        put_mat(bw, carry, j)
        return carry

    def gw_step(i, carry):
        j = J - 2 - i
        moved = mat_mat(mat_rows(upp, j), carry)
        carry = mat_map(lambda a, b: a - b, get_mat(fw, j), moved)
        put_mat(gw, carry, j)
        return carry

    first_b = lax.fori_loop(0, J - 1, bw_step, start_b)
    first_g = lax.fori_loop(0, J - 1, gw_step, last_f)

    steps = (1, 2, 4)
    whole = last_f
    for level, s in enumerate(steps):
        put_mat(scan_f, mat_map(lambda a: jnp.where(chunk >= s, a, 0.0), whole), level)
        moved = mat_mat(whole, mat_map(lambda a: pltpu.roll(a, s, 0), whole))
        whole = mat_map(lambda a, b: jnp.where(chunk >= s, b, a), whole, moved)
    before = mat_map(lambda a: pltpu.roll(a, 1, 0), whole)
    before = [[jnp.where(chunk >= 1, before[c][e], 1.0 if c == e else 0.0) for e in range(N)] for c in range(N)]
    put_mat(excl, before, 0)
    for c in range(N):
        for e in range(N):
            map_all[me, pl.ds(c * N + e, 1), :] = whole[c][e][K - 1:K]
    seen = mat_mat(first_g, before)
    put_mat(excl, seen, 1)

    whole = first_b
    for level, s in enumerate(steps):
        put_mat(scan_b, mat_map(lambda a: jnp.where(chunk < K - s, a, 0.0), whole), level)
        moved = mat_mat(whole, mat_map(lambda a: pltpu.roll(a, K - s, 0), whole))
        whole = mat_map(lambda a, b: jnp.where(chunk < K - s, b, a), whole, moved)
    after = mat_map(lambda a: pltpu.roll(a, K - 1, 0), whole)
    after = [[jnp.where(chunk < K - 1, after[c][e], 1.0 if c == e else 0.0) for e in range(N)] for c in range(N)]
    put_mat(excl, after, 2)
    for c in range(N):
        for e in range(N):
            map_all[me, pl.ds(N * N + c * N + e, 1), :] = whole[c][e][0:1]
    seen = get_mat(excl, 1)
    for level, s in enumerate(steps):
        moved = mat_mat(get_mat(scan_b, level), mat_map(lambda a: pltpu.roll(a, K - s, 0), seen))
        seen = mat_map(jnp.add, seen, moved)
    for c in range(N):
        for e in range(N):
            map_all[me, pl.ds(2 * N * N + c * N + e, 1), :] = seen[c][e][0:1]
    put_mat(excl, mat_map(lambda a: jnp.where(chunk < K - 1, pltpu.roll(a, K - 1, 0), 0.0), seen), 1)
    map_now = normal_copies(map_all, map_send, map_recv)
    for copy in map_now:
        copy.start()
    pending += map_now

    for sweep in range(SWEEPS):
        here = xb.at[sweep]
        if sweep == 0:
            ld_don.wait()
        places = [don[pl.ds(j, K, stride=J), :] for j in range(J)]
        row_of = [p // LANES for p in places]
        col_of = [p % LANES for p in places]

        def gather_step(r, carry):
            out = []
            rows = [jnp.broadcast_to(here[pl.ds(r * N + c, 1), :], (K, LANES)) for c in range(N)]
            for j in range(J):
                hit = row_of[j] == r
                for c in range(N):
                    got = jnp.take_along_axis(rows[c], col_of[j], axis=1, mode="promise_in_bounds")
                    out.append(jnp.where(hit, got, carry[j * N + c]))
            return out

        got = lax.fori_loop(0, J * K, gather_step, [jnp.zeros((K, LANES), jnp.float32)] * (J * N))
        for i in range(J * N):
            donated[i] = got[i]

        if sweep == 0:
            for load in (ld_src, ld_ibl, ld_cpl):
                load.wait()
        for copy in edge_now:
            copy.wait_recv()
        left = edge_in[sweep, 0]
        right = edge_in[sweep, sides_stream - 1]
        lows, highs = [], []
        for j in range(J):
            rows = vec_rows(here, j)
            flag = ibl[pl.ds(j, K, stride=J), :]
            lows, highs = [], []
            for c in range(N):
                i = j * N + c
                lows.append(jnp.where(lane == 0, pltpu.roll(left, (LANES - 2 * i) % LANES, 1), pltpu.roll(rows[c], 1, 1)))
                highs.append(jnp.where(lane == LANES - 1, pltpu.roll(right, LANES - 2 - 2 * i, 1), pltpu.roll(rows[c], LANES - 1, 1)))
            c2 = mat_rows(cpl, j, 2 * J * K * N * N)
            c3 = mat_rows(cpl, j, 3 * J * K * N * N)
            s_rows = vec_rows(src, j)
            for c in range(N):
                acc = s_rows[c] + jnp.where(flag == 2, donated[j * N + c], 0.0)
                for e in range(N):
                    acc = acc - (c2[e][c] * lows[e] + c3[e][c] * highs[e])
                base[j * N + c] = acc

        for copy in span_now:
            copy.wait_recv()
        if sweep == 0:
            ld_piv.wait()

        def forward_step(j, state):
            c0 = mat_rows(cpl, j)
            c1 = mat_rows(cpl, j, J * K * N * N)
            flag = ibl[pl.ds(j, K, stride=J), :]
            x0 = vec_rows(plane.at[sweep, 0], j)
            rhs = []
            if sides_span == 1:
                both = mat_map(jnp.add, c0, c1)
                for c in range(N):
                    acc = functools.reduce(jnp.add, [both[e][c] * x0[e] for e in range(N)])
                    rhs.append(jnp.where(flag == 0, 0.0, base[j * N + c] - acc))
            else:
                x1 = vec_rows(plane.at[sweep, 1], j)
                for c in range(N):
                    acc = functools.reduce(jnp.add, [c0[e][c] * x0[e] + c1[e][c] * x1[e] for e in range(N)])
                    rhs.append(jnp.where(flag == 0, 0.0, base[j * N + c] - acc))
            scaled = mat_vec(mat_rows(piv, j), rhs)
            moved = mat_vec(mat_rows(low, j), state)
            state = [a - b for a, b in zip(scaled, moved)]
            for c in range(N):
                work[j * N + c] = state[c]
            return state

        zero = [jnp.zeros((K, LANES), jnp.float32)] * N
        f = lax.fori_loop(0, J, forward_step, zero)

        def backward_step(i, state):
            j = J - 1 - i
            moved = mat_vec(mat_rows(upp, j), state)
            state = [work[j * N + c] - moved[c] for c in range(N)]
            for c in range(N):
                work[j * N + c] = state[c]
            return state

        b = lax.fori_loop(0, J, backward_step, zero)
        for level, s in enumerate(steps):
            f = vec_add(f, mat_vec(get_mat(scan_f, level), [pltpu.roll(v, s, 0) for v in f]))
        y_in = [jnp.where(chunk >= 1, pltpu.roll(v, 1, 0), 0.0) for v in f]
        b = vec_add(b, mat_vec(get_mat(gw, 0), y_in))
        for level, s in enumerate(steps):
            b = vec_add(b, mat_vec(get_mat(scan_b, level), [pltpu.roll(v, K - s, 0) for v in b]))
        x_in = [jnp.where(chunk < K - 1, pltpu.roll(v, K - 1, 0), 0.0) for v in b]
        for c in range(N):
            vec_all[sweep, me, pl.ds(c, 1), :] = f[c][K - 1:K]
            vec_all[sweep, me, pl.ds(K + c, 1), :] = b[c][0:1]
        sends = normal_copies(vec_all.at[sweep], vec_send.at[sweep], vec_recv.at[sweep])
        for copy in sends:
            copy.start()
        pending += sends
        if sweep == 0:
            for copy in normal_arrivals(map_all, map_send, map_recv):
                copy.wait_recv()
        for copy in normal_arrivals(vec_all.at[sweep], vec_send.at[sweep], vec_recv.at[sweep]):
            copy.wait_recv()

        def apply_map(d, m, state):
            return functools.reduce(jnp.add, [
                map_all[d, pl.ds(m * N * N + e, N, stride=N), :] * state[e:e + 1] for e in range(N)])

        none = jnp.zeros((N, LANES), jnp.float32)
        entries, state, mine = [none], none, none
        for d in range(n_normal - 1):
            state = vec_all[sweep, d, pl.ds(0, N), :] + apply_map(d, 0, state)
            entries.append(state)
            mine = jnp.where(me == d + 1, state, mine)
        x_state, x_mine = none, none
        for d in range(n_normal - 1, 0, -1):
            x_state = (vec_all[sweep, d, pl.ds(K, N), :] + apply_map(d, 2, entries[d])) + apply_map(d, 1, x_state)
            x_mine = jnp.where(me == d - 1, x_state, x_mine)
        y_entry = [jnp.broadcast_to(mine[c:c + 1], (K, LANES)) for c in range(N)]
        x_entry = [jnp.broadcast_to(x_mine[c:c + 1], (K, LANES)) for c in range(N)]
        y_in = vec_add(y_in, mat_vec(get_mat(excl, 0), y_entry))
        x_in = vec_add(x_in, mat_vec(get_mat(excl, 1), y_entry))
        x_in = vec_add(x_in, mat_vec(get_mat(excl, 2), x_entry))

        target = out_ref if sweep == SWEEPS - 1 else xb.at[sweep + 1]

        def final_step(j, carry):
            more = vec_add(mat_vec(get_mat(gw, j), y_in), mat_vec(get_mat(bw, j), x_in))
            for c in range(N):
                target[pl.ds(j * N + c, K, stride=J * N), :] = work[j * N + c] + more[c]
            return carry

        lax.fori_loop(0, J, final_step, 0)
        if sweep < SWEEPS - 1:
            span_now = span_copies(sweep + 1, xb.at[sweep + 1])
            for copy in span_now:
                copy.start()
            edge_now = send_edges(sweep + 1)
            pending += list(span_now) + list(edge_now)

    for copy in pending:
        copy.wait_send()


def per_device(sizes, iterate, source, pivot, lower, upper, coupling, iblank, donor):
    points, comps, planes, lines = iterate.shape
    n_normal, n_span, n_stream = sizes
    J = points // K
    rows, mats = points * N, points * N * N
    sides_span, sides_stream = (1 if n_span == 2 else 2), (1 if n_stream == 2 else 2)
    f32 = jnp.float32
    peers = max(n_normal - 1, 1)
    scratch = [
        pltpu.VMEM((SWEEPS, rows, LANES), f32),
        pltpu.VMEM((rows, LANES), f32),
        pltpu.VMEM((mats, LANES), f32),
        pltpu.VMEM((mats, LANES), f32),
        pltpu.VMEM((mats, LANES), f32),
        pltpu.VMEM((4 * mats, LANES), f32),
        pltpu.VMEM((points, LANES), jnp.int32),
        pltpu.VMEM((points, LANES), jnp.int32),
        pltpu.VMEM((SWEEPS, sides_span, rows, LANES), f32),
        pltpu.VMEM((SWEEPS, K, LANES), f32),
        pltpu.VMEM((SWEEPS, sides_stream, K, LANES), f32),
        pltpu.VMEM((SWEEPS, n_normal, 2 * K, LANES), f32),
        pltpu.VMEM((n_normal, 80, LANES), f32),
        pltpu.VMEM((J, N, N, K, LANES), f32),
        pltpu.VMEM((J, N, N, K, LANES), f32),
        pltpu.VMEM((J, N, N, K, LANES), f32),
        pltpu.VMEM((3, N, N, K, LANES), f32),
        pltpu.VMEM((3, N, N, K, LANES), f32),
        pltpu.VMEM((3, N, N, K, LANES), f32),
        pltpu.VMEM((J * N, K, LANES), f32),
        pltpu.VMEM((J * N, K, LANES), f32),
        pltpu.VMEM((J * N, K, LANES), f32),
        pltpu.SemaphoreType.DMA((8,)),
        pltpu.SemaphoreType.DMA((SWEEPS, sides_span)),
        pltpu.SemaphoreType.DMA((SWEEPS, sides_span)),
        pltpu.SemaphoreType.DMA((SWEEPS, sides_stream)),
        pltpu.SemaphoreType.DMA((SWEEPS, sides_stream)),
        pltpu.SemaphoreType.DMA((SWEEPS, peers)),
        pltpu.SemaphoreType.DMA((SWEEPS, peers)),
        pltpu.SemaphoreType.DMA((peers,)),
        pltpu.SemaphoreType.DMA((peers,)),
    ]
    out = pl.pallas_call(
        functools.partial(kernel, sizes, J),
        out_shape=jax.ShapeDtypeStruct((rows, LANES), f32),
        in_specs=[pl.BlockSpec(memory_space=pl.ANY)] * 8,
        out_specs=pl.BlockSpec(memory_space=pltpu.VMEM),
        scratch_shapes=scratch,
        compiler_params=pltpu.CompilerParams(
            collective_id=0, has_side_effects=True, vmem_limit_bytes=32 * 1024 * 1024),
        cost_estimate=pl.CostEstimate(flops=12000000, bytes_accessed=5000000, transcendentals=0),
    )(
        iterate.reshape(rows, lines), source.reshape(rows, lines), pivot.reshape(mats, lines),
        lower.reshape(mats, lines), upper.reshape(mats, lines), coupling.reshape(4 * mats, lines),
        iblank.reshape(points, lines), donor.reshape(points, lines),
    )
    return out.reshape(points, comps, planes, lines)


def solution(mesh):
    placed = (
        P("normal", None, "span", "stream"),
        P("normal", None, "span", "stream"),
        P("normal", None, None, "span", "stream"),
        P("normal", None, None, "span", "stream"),
        P("normal", None, None, "span", "stream"),
        P(None, "normal", None, None, "span", "stream"),
        P("normal", "span", "stream"),
        P("normal", "span", "stream"),
    )
    sizes = tuple(mesh.shape[name] for name in ("normal", "span", "stream"))
    return jax.shard_map(
        functools.partial(per_device, sizes),
        mesh=mesh,
        in_specs=placed,
        out_specs=P("normal", None, "span", "stream"),
        check_vma=False,
    )
```

```python
import functools
import jax
import jax.numpy as jnp
from jax import lax
from jax.experimental import pallas as pl
from jax.experimental.pallas import tpu as pltpu
from jax.sharding import PartitionSpec as P

SWEEPS = 2
N = 5
K = 8
LANES = 128
MESH = pl.DeviceIdType.MESH


def mat_vec(mat, vec):
    return [functools.reduce(jnp.add, [mat[c][e] * vec[e] for e in range(N)]) for c in range(N)]


def mat_mat(left, right):
    return [
        [functools.reduce(jnp.add, [left[c][e] * right[e][f] for e in range(N)]) for f in range(N)]
        for c in range(N)
    ]


def mat_map(function, *mats):
    return [[function(*(m[c][e] for m in mats)) for e in range(N)] for c in range(N)]


def vec_add(a, b):
    return [p + q for p, q in zip(a, b)]


def lane_gather(row, index):
    numbers = lax.GatherDimensionNumbers(
        offset_dims=(), collapsed_slice_dims=(1,), start_index_map=(1,),
        operand_batching_dims=(0,), start_indices_batching_dims=(0,))
    return lax.gather(row, index[..., None], numbers, (1, 1), mode=lax.GatherScatterMode.PROMISE_IN_BOUNDS)


def kernel(sizes, per_chunk, x_hbm, src_hbm, piv_hbm, low_hbm, upp_hbm, cpl_hbm, ibl_hbm, don_hbm, out_ref,
           xb, src, piv, low, upp, cpl, ibl, don, plane, edge_out, edge_in, vec_all, map_all,
           fw, gw, bw, scan_f, scan_b, excl, base, work, donated,
           load_sem, span_send, span_recv, edge_send, edge_recv, vec_send, vec_recv, map_send, map_recv):
    J = per_chunk
    n_normal, n_span, n_stream = sizes
    me, sp, st = lax.axis_index("normal"), lax.axis_index("span"), lax.axis_index("stream")
    span_targets = [lax.rem(sp + 1, n_span)] if n_span == 2 else [lax.rem(sp + 1, n_span), lax.rem(sp + n_span - 1, n_span)]
    stream_targets = [lax.rem(st + 1, n_stream)] if n_stream == 2 else [lax.rem(st + 1, n_stream), lax.rem(st + n_stream - 1, n_stream)]
    sides_span, sides_stream = len(span_targets), len(stream_targets)

    pairs = [(x_hbm, xb.at[0]), (low_hbm, low), (upp_hbm, upp), (don_hbm, don), (cpl_hbm, cpl),
             (src_hbm, src), (ibl_hbm, ibl), (piv_hbm, piv)]
    loads = [pltpu.make_async_copy(a, b, load_sem.at[i]) for i, (a, b) in enumerate(pairs)]
    for load in loads:
        load.start()
    ld_x, ld_low, ld_upp, ld_don, ld_cpl, ld_src, ld_ibl, ld_piv = loads

    barrier = pltpu.get_barrier_semaphore()
    for t in span_targets:
        pl.semaphore_signal(barrier, inc=1, device_id={"span": t}, device_id_type=MESH)
    for t in stream_targets:
        pl.semaphore_signal(barrier, inc=1, device_id={"stream": t}, device_id_type=MESH)
    for o in range(1, n_normal):
        pl.semaphore_signal(barrier, inc=1, device_id={"normal": lax.rem(me + o, n_normal)}, device_id_type=MESH)
    pl.semaphore_wait(barrier, sides_span + sides_stream + n_normal - 1)

    def span_copies(sweep, source):
        return [
            pltpu.make_async_remote_copy(
                src_ref=source, dst_ref=plane.at[sweep, i], send_sem=span_send.at[sweep, i],
                recv_sem=span_recv.at[sweep, i], device_id={"span": t}, device_id_type=MESH)
            for i, t in enumerate(span_targets)
        ]

    def edge_copies(sweep):
        return [
            pltpu.make_async_remote_copy(
                src_ref=edge_out.at[sweep], dst_ref=edge_in.at[sweep, i], send_sem=edge_send.at[sweep, i],
                recv_sem=edge_recv.at[sweep, i], device_id={"stream": t}, device_id_type=MESH)
            for i, t in enumerate(stream_targets)
        ]

    def normal_copies(ref, sends, recvs):
        out = []
        for o in range(1, n_normal):
            out.append(pltpu.make_async_remote_copy(
                src_ref=ref.at[me], dst_ref=ref.at[me], send_sem=sends.at[o - 1], recv_sem=recvs.at[o - 1],
                device_id={"normal": lax.rem(me + o, n_normal)}, device_id_type=MESH))
        return out

    def normal_arrivals(ref, sends, recvs):
        out = []
        for o in range(1, n_normal):
            came = lax.rem(me + n_normal - o, n_normal)
            out.append(pltpu.make_async_remote_copy(
                src_ref=ref.at[me], dst_ref=ref.at[came], send_sem=sends.at[o - 1], recv_sem=recvs.at[o - 1],
                device_id={"normal": lax.rem(me + o, n_normal)}, device_id_type=MESH))
        return out

    lane = lax.broadcasted_iota(jnp.int32, (K, LANES), 1)
    chunk = lax.broadcasted_iota(jnp.int32, (K, LANES), 0)

    def vec_rows(ref, j):
        return [ref[pl.ds(j * N + c, K, stride=J * N), :] for c in range(N)]

    def mat_rows(ref, j, first=0):
        return [[ref[pl.ds(first + j * N * N + c * N + e, K, stride=J * N * N), :] for e in range(N)] for c in range(N)]

    def get_mat(ref, *at):
        return [[ref[(*at, c, e)] for e in range(N)] for c in range(N)]

    def put_mat(ref, mat, *at):
        for c in range(N):
            for e in range(N):
                ref[(*at, c, e)] = mat[c][e]

    def send_edges(sweep):
        packed = jnp.zeros((K, LANES), jnp.float32)
        for j in range(J):
            rows = vec_rows(xb.at[sweep], j)
            for c in range(N):
                i = j * N + c
                packed = jnp.where(lane >> 1 == i, pltpu.roll(rows[c], 2 * i + 1, 1), packed)
        edge_out[sweep] = packed
        copies = edge_copies(sweep)
        for copy in copies:
            copy.start()
        return copies

    span_now = span_copies(0, x_hbm)
    for copy in span_now:
        copy.start()
    ld_x.wait()
    edge_now = send_edges(0)
    pending = list(span_now) + list(edge_now)

    ld_low.wait()
    ld_upp.wait()

    first = mat_map(lambda a: -a, mat_rows(low, 0))
    put_mat(fw, first, 0)

    def fw_step(j, carry):
        carry = mat_mat(mat_map(lambda a: -a, mat_rows(low, j)), carry)
        put_mat(fw, carry, j)
        return carry

    last_f = lax.fori_loop(1, J, fw_step, first)
    start_b = mat_map(lambda a: -a, mat_rows(upp, J - 1))
    put_mat(bw, start_b, J - 1)
    put_mat(gw, last_f, J - 1)

    def bw_step(i, carry):
        j = J - 2 - i
        carry = mat_mat(mat_map(lambda a: -a, mat_rows(upp, j)), carry)
        put_mat(bw, carry, j)
        return carry

    def gw_step(i, carry):
        j = J - 2 - i
        moved = mat_mat(mat_rows(upp, j), carry)
        carry = mat_map(lambda a, b: a - b, get_mat(fw, j), moved)
        put_mat(gw, carry, j)
        return carry

    first_b = lax.fori_loop(0, J - 1, bw_step, start_b)
    first_g = lax.fori_loop(0, J - 1, gw_step, last_f)

    steps = (1, 2, 4)
    whole = last_f
    for level, s in enumerate(steps):
        put_mat(scan_f, mat_map(lambda a: jnp.where(chunk >= s, a, 0.0), whole), level)
        moved = mat_mat(whole, mat_map(lambda a: pltpu.roll(a, s, 0), whole))
        whole = mat_map(lambda a, b: jnp.where(chunk >= s, b, a), whole, moved)
    before = mat_map(lambda a: pltpu.roll(a, 1, 0), whole)
    before = [[jnp.where(chunk >= 1, before[c][e], 1.0 if c == e else 0.0) for e in range(N)] for c in range(N)]
    put_mat(excl, before, 0)
    for c in range(N):
        for e in range(N):
            map_all[me, pl.ds(c * N + e, 1), :] = whole[c][e][K - 1:K]
    seen = mat_mat(first_g, before)
    put_mat(excl, seen, 1)

    whole = first_b
    for level, s in enumerate(steps):
        put_mat(scan_b, mat_map(lambda a: jnp.where(chunk < K - s, a, 0.0), whole), level)
        moved = mat_mat(whole, mat_map(lambda a: pltpu.roll(a, K - s, 0), whole))
        whole = mat_map(lambda a, b: jnp.where(chunk < K - s, b, a), whole, moved)
    after = mat_map(lambda a: pltpu.roll(a, K - 1, 0), whole)
    after = [[jnp.where(chunk < K - 1, after[c][e], 1.0 if c == e else 0.0) for e in range(N)] for c in range(N)]
    put_mat(excl, after, 2)
    for c in range(N):
        for e in range(N):
            map_all[me, pl.ds(N * N + c * N + e, 1), :] = whole[c][e][0:1]
    seen = get_mat(excl, 1)
    for level, s in enumerate(steps):
        moved = mat_mat(get_mat(scan_b, level), mat_map(lambda a: pltpu.roll(a, K - s, 0), seen))
        seen = mat_map(jnp.add, seen, moved)
    for c in range(N):
        for e in range(N):
            map_all[me, pl.ds(2 * N * N + c * N + e, 1), :] = seen[c][e][0:1]
    put_mat(excl, mat_map(lambda a: jnp.where(chunk < K - 1, pltpu.roll(a, K - 1, 0), 0.0), seen), 1)
    map_now = normal_copies(map_all, map_send, map_recv)
    for copy in map_now:
        copy.start()
    pending += map_now

    for sweep in range(SWEEPS):
        here = xb.at[sweep]
        if sweep == 0:
            ld_don.wait()
        places = [don[pl.ds(j, K, stride=J), :] for j in range(J)]
        row_of = [p >> 7 for p in places]
        col_of = [p & (LANES - 1) for p in places]

        def gather_step(r, carry):
            out = []
            rows = [jnp.broadcast_to(here[pl.ds(r * N + c, 1), :], (K, LANES)) for c in range(N)]
            for j in range(J):
                hit = row_of[j] == r
                for c in range(N):
                    got = lane_gather(rows[c], col_of[j])
                    out.append(jnp.where(hit, got, carry[j * N + c]))
            return out

        got = lax.fori_loop(0, J * K, gather_step, [jnp.zeros((K, LANES), jnp.float32)] * (J * N), unroll=8)
        for i in range(J * N):
            donated[i] = got[i]

        if sweep == 0:
            for load in (ld_src, ld_ibl, ld_cpl):
                load.wait()
        for copy in edge_now:
            copy.wait_recv()
        left = edge_in[sweep, 0]
        right = edge_in[sweep, sides_stream - 1]
        lows, highs = [], []
        for j in range(J):
            rows = vec_rows(here, j)
            flag = ibl[pl.ds(j, K, stride=J), :]
            lows, highs = [], []
            for c in range(N):
                i = j * N + c
                lows.append(jnp.where(lane == 0, pltpu.roll(left, (LANES - 2 * i) % LANES, 1), pltpu.roll(rows[c], 1, 1)))
                highs.append(jnp.where(lane == LANES - 1, pltpu.roll(right, LANES - 2 - 2 * i, 1), pltpu.roll(rows[c], LANES - 1, 1)))
            c2 = mat_rows(cpl, j, 2 * J * K * N * N)
            c3 = mat_rows(cpl, j, 3 * J * K * N * N)
            s_rows = vec_rows(src, j)
            for c in range(N):
                acc = s_rows[c] + jnp.where(flag == 2, donated[j * N + c], 0.0)
                for e in range(N):
                    acc = acc - (c2[e][c] * lows[e] + c3[e][c] * highs[e])
                base[j * N + c] = acc

        for copy in span_now:
            copy.wait_recv()
        if sweep == 0:
            ld_piv.wait()

        def forward_step(j, state):
            c0 = mat_rows(cpl, j)
            c1 = mat_rows(cpl, j, J * K * N * N)
            flag = ibl[pl.ds(j, K, stride=J), :]
            x0 = vec_rows(plane.at[sweep, 0], j)
            rhs = []
            if sides_span == 1:
                both = mat_map(jnp.add, c0, c1)
                for c in range(N):
                    acc = functools.reduce(jnp.add, [both[e][c] * x0[e] for e in range(N)])
                    rhs.append(jnp.where(flag == 0, 0.0, base[j * N + c] - acc))
            else:
                x1 = vec_rows(plane.at[sweep, 1], j)
                for c in range(N):
                    acc = functools.reduce(jnp.add, [c0[e][c] * x0[e] + c1[e][c] * x1[e] for e in range(N)])
                    rhs.append(jnp.where(flag == 0, 0.0, base[j * N + c] - acc))
            scaled = mat_vec(mat_rows(piv, j), rhs)
            moved = mat_vec(mat_rows(low, j), state)
            state = [a - b for a, b in zip(scaled, moved)]
            for c in range(N):
                work[j * N + c] = state[c]
            return state

        zero = [jnp.zeros((K, LANES), jnp.float32)] * N
        f = lax.fori_loop(0, J, forward_step, zero, unroll=True)

        def backward_step(i, state):
            j = J - 1 - i
            moved = mat_vec(mat_rows(upp, j), state)
            state = [work[j * N + c] - moved[c] for c in range(N)]
            for c in range(N):
                work[j * N + c] = state[c]
            return state

        b = lax.fori_loop(0, J, backward_step, zero, unroll=True)
        for level, s in enumerate(steps):
            f = vec_add(f, mat_vec(get_mat(scan_f, level), [pltpu.roll(v, s, 0) for v in f]))
        y_in = [jnp.where(chunk >= 1, pltpu.roll(v, 1, 0), 0.0) for v in f]
        b = vec_add(b, mat_vec(get_mat(gw, 0), y_in))
        for level, s in enumerate(steps):
            b = vec_add(b, mat_vec(get_mat(scan_b, level), [pltpu.roll(v, K - s, 0) for v in b]))
        x_in = [jnp.where(chunk < K - 1, pltpu.roll(v, K - 1, 0), 0.0) for v in b]
        for c in range(N):
            vec_all[sweep, me, pl.ds(c, 1), :] = f[c][K - 1:K]
            vec_all[sweep, me, pl.ds(K + c, 1), :] = b[c][0:1]
        sends = normal_copies(vec_all.at[sweep], vec_send.at[sweep], vec_recv.at[sweep])
        for copy in sends:
            copy.start()
        pending += sends
        if sweep == 0:
            for copy in normal_arrivals(map_all, map_send, map_recv):
                copy.wait_recv()
        for copy in normal_arrivals(vec_all.at[sweep], vec_send.at[sweep], vec_recv.at[sweep]):
            copy.wait_recv()

        def apply_map(d, m, state):
            return functools.reduce(jnp.add, [
                map_all[d, pl.ds(m * N * N + e, N, stride=N), :] * state[e:e + 1] for e in range(N)])

        none = jnp.zeros((N, LANES), jnp.float32)
        entries, state, mine = [none], none, none
        for d in range(n_normal - 1):
            state = vec_all[sweep, d, pl.ds(0, N), :] + apply_map(d, 0, state)
            entries.append(state)
            mine = jnp.where(me == d + 1, state, mine)
        x_state, x_mine = none, none
        for d in range(n_normal - 1, 0, -1):
            x_state = (vec_all[sweep, d, pl.ds(K, N), :] + apply_map(d, 2, entries[d])) + apply_map(d, 1, x_state)
            x_mine = jnp.where(me == d - 1, x_state, x_mine)
        y_entry = [jnp.broadcast_to(mine[c:c + 1], (K, LANES)) for c in range(N)]
        x_entry = [jnp.broadcast_to(x_mine[c:c + 1], (K, LANES)) for c in range(N)]
        y_in = vec_add(y_in, mat_vec(get_mat(excl, 0), y_entry))
        x_in = vec_add(x_in, mat_vec(get_mat(excl, 1), y_entry))
        x_in = vec_add(x_in, mat_vec(get_mat(excl, 2), x_entry))

        target = out_ref if sweep == SWEEPS - 1 else xb.at[sweep + 1]

        def final_step(j, carry):
            more = vec_add(mat_vec(get_mat(gw, j), y_in), mat_vec(get_mat(bw, j), x_in))
            for c in range(N):
                target[pl.ds(j * N + c, K, stride=J * N), :] = work[j * N + c] + more[c]
            return carry

        lax.fori_loop(0, J, final_step, 0, unroll=True)
        if sweep < SWEEPS - 1:
            span_now = span_copies(sweep + 1, xb.at[sweep + 1])
            for copy in span_now:
                copy.start()
            edge_now = send_edges(sweep + 1)
            pending += list(span_now) + list(edge_now)

    for copy in pending:
        copy.wait_send()


def per_device(sizes, iterate, source, pivot, lower, upper, coupling, iblank, donor):
    points, comps, planes, lines = iterate.shape
    n_normal, n_span, n_stream = sizes
    J = points // K
    rows, mats = points * N, points * N * N
    sides_span, sides_stream = (1 if n_span == 2 else 2), (1 if n_stream == 2 else 2)
    f32 = jnp.float32
    peers = max(n_normal - 1, 1)
    scratch = [
        pltpu.VMEM((SWEEPS, rows, LANES), f32),
        pltpu.VMEM((rows, LANES), f32),
        pltpu.VMEM((mats, LANES), f32),
        pltpu.VMEM((mats, LANES), f32),
        pltpu.VMEM((mats, LANES), f32),
        pltpu.VMEM((4 * mats, LANES), f32),
        pltpu.VMEM((points, LANES), jnp.int32),
        pltpu.VMEM((points, LANES), jnp.int32),
        pltpu.VMEM((SWEEPS, sides_span, rows, LANES), f32),
        pltpu.VMEM((SWEEPS, K, LANES), f32),
        pltpu.VMEM((SWEEPS, sides_stream, K, LANES), f32),
        pltpu.VMEM((SWEEPS, n_normal, 2 * K, LANES), f32),
        pltpu.VMEM((n_normal, 80, LANES), f32),
        pltpu.VMEM((J, N, N, K, LANES), f32),
        pltpu.VMEM((J, N, N, K, LANES), f32),
        pltpu.VMEM((J, N, N, K, LANES), f32),
        pltpu.VMEM((3, N, N, K, LANES), f32),
        pltpu.VMEM((3, N, N, K, LANES), f32),
        pltpu.VMEM((3, N, N, K, LANES), f32),
        pltpu.VMEM((J * N, K, LANES), f32),
        pltpu.VMEM((J * N, K, LANES), f32),
        pltpu.VMEM((J * N, K, LANES), f32),
        pltpu.SemaphoreType.DMA((8,)),
        pltpu.SemaphoreType.DMA((SWEEPS, sides_span)),
        pltpu.SemaphoreType.DMA((SWEEPS, sides_span)),
        pltpu.SemaphoreType.DMA((SWEEPS, sides_stream)),
        pltpu.SemaphoreType.DMA((SWEEPS, sides_stream)),
        pltpu.SemaphoreType.DMA((SWEEPS, peers)),
        pltpu.SemaphoreType.DMA((SWEEPS, peers)),
        pltpu.SemaphoreType.DMA((peers,)),
        pltpu.SemaphoreType.DMA((peers,)),
    ]
    out = pl.pallas_call(
        functools.partial(kernel, sizes, J),
        out_shape=jax.ShapeDtypeStruct((rows, LANES), f32),
        in_specs=[pl.BlockSpec(memory_space=pltpu.HBM)] * 8,
        out_specs=pl.BlockSpec(memory_space=pltpu.VMEM),
        scratch_shapes=scratch,
        compiler_params=pltpu.CompilerParams(
            collective_id=0, has_side_effects=True, vmem_limit_bytes=62 * 1024 * 1024),
        cost_estimate=pl.CostEstimate(flops=12000000, bytes_accessed=5000000, transcendentals=0),
    )(
        iterate.reshape(rows, lines), source.reshape(rows, lines), pivot.reshape(mats, lines),
        lower.reshape(mats, lines), upper.reshape(mats, lines), coupling.reshape(4 * mats, lines),
        iblank.reshape(points, lines), donor.reshape(points, lines),
    )
    return out.reshape(points, comps, planes, lines)


def solution(mesh):
    placed = (
        P("normal", None, "span", "stream"),
        P("normal", None, "span", "stream"),
        P("normal", None, None, "span", "stream"),
        P("normal", None, None, "span", "stream"),
        P("normal", None, None, "span", "stream"),
        P(None, "normal", None, None, "span", "stream"),
        P("normal", "span", "stream"),
        P("normal", "span", "stream"),
    )
    sizes = tuple(mesh.shape[name] for name in ("normal", "span", "stream"))
    return jax.shard_map(
        functools.partial(per_device, sizes),
        mesh=mesh,
        in_specs=placed,
        out_specs=P("normal", None, "span", "stream"),
        check_vma=False,
    )
```

```python
import functools
import jax
import jax.numpy as jnp
from jax import lax
from jax.experimental import pallas as pl
from jax.experimental.pallas import tpu as pltpu
from jax.sharding import PartitionSpec as P

SWEEPS = 2
N = 5
K = 8
LANES = 128
MESH = pl.DeviceIdType.MESH


def mat_vec(mat, vec):
    return [functools.reduce(jnp.add, [mat[c][e] * vec[e] for e in range(N)]) for c in range(N)]


def mat_mat(left, right):
    return [
        [functools.reduce(jnp.add, [left[c][e] * right[e][f] for e in range(N)]) for f in range(N)]
        for c in range(N)
    ]


def mat_map(function, *mats):
    return [[function(*(m[c][e] for m in mats)) for e in range(N)] for c in range(N)]


def vec_add(a, b):
    return [p + q for p, q in zip(a, b)]


def lane_gather(row, index):
    numbers = lax.GatherDimensionNumbers(
        offset_dims=(), collapsed_slice_dims=(1,), start_index_map=(1,),
        operand_batching_dims=(0,), start_indices_batching_dims=(0,))
    return lax.gather(row, index[..., None], numbers, (1, 1), mode=lax.GatherScatterMode.PROMISE_IN_BOUNDS)


def kernel(sizes, per_chunk, x_hbm, src_hbm, piv_hbm, low_hbm, upp_hbm, cpl_hbm, ibl_hbm, don_hbm, out_ref,
           xb, xk, src, piv, low, upp, cpl, ibl, don, plane, plane_k, edge_out, edge_in, vec_all, map_all,
           fw, gw, bw, scan_f, scan_b, excl, base, work, donated,
           load_sem, span_send, span_recv, piece_send, piece_recv, edge_send, edge_recv, vec_send, vec_recv, map_send, map_recv):
    J = per_chunk
    n_normal, n_span, n_stream = sizes
    me, sp, st = lax.axis_index("normal"), lax.axis_index("span"), lax.axis_index("stream")
    span_targets = [lax.rem(sp + 1, n_span)] if n_span == 2 else [lax.rem(sp + 1, n_span), lax.rem(sp + n_span - 1, n_span)]
    stream_targets = [lax.rem(st + 1, n_stream)] if n_stream == 2 else [lax.rem(st + 1, n_stream), lax.rem(st + n_stream - 1, n_stream)]
    sides_span, sides_stream = len(span_targets), len(stream_targets)

    pairs = [(x_hbm, xb), (low_hbm, low), (upp_hbm, upp), (don_hbm, don), (cpl_hbm, cpl),
             (src_hbm, src), (ibl_hbm, ibl), (piv_hbm, piv)]
    loads = [pltpu.make_async_copy(a, b, load_sem.at[i]) for i, (a, b) in enumerate(pairs)]
    for load in loads:
        load.start()
    ld_x, ld_low, ld_upp, ld_don, ld_cpl, ld_src, ld_ibl, ld_piv = loads

    barrier = pltpu.get_barrier_semaphore()
    for t in span_targets:
        pl.semaphore_signal(barrier, inc=1, device_id={"span": t}, device_id_type=MESH)
    for t in stream_targets:
        pl.semaphore_signal(barrier, inc=1, device_id={"stream": t}, device_id_type=MESH)
    for o in range(1, n_normal):
        pl.semaphore_signal(barrier, inc=1, device_id={"normal": lax.rem(me + o, n_normal)}, device_id_type=MESH)
    pl.semaphore_wait(barrier, sides_span + sides_stream + n_normal - 1)

    def span_copies():
        return [
            pltpu.make_async_remote_copy(
                src_ref=x_hbm, dst_ref=plane.at[i], send_sem=span_send.at[i],
                recv_sem=span_recv.at[i], device_id={"span": t}, device_id_type=MESH)
            for i, t in enumerate(span_targets)
        ]

    group = 2 if J % 2 == 0 else 1

    def piece_copies(sweep, piece):
        part = pl.ds(piece * group * N, group * N)
        return [
            pltpu.make_async_remote_copy(
                src_ref=xk.at[sweep - 1, part], dst_ref=plane_k.at[sweep - 1, i, part],
                send_sem=piece_send.at[sweep - 1, piece, i], recv_sem=piece_recv.at[sweep - 1, piece, i],
                device_id={"span": t}, device_id_type=MESH)
            for i, t in enumerate(span_targets)
        ]

    def edge_copies(sweep):
        return [
            pltpu.make_async_remote_copy(
                src_ref=edge_out.at[sweep], dst_ref=edge_in.at[sweep, i], send_sem=edge_send.at[sweep, i],
                recv_sem=edge_recv.at[sweep, i], device_id={"stream": t}, device_id_type=MESH)
            for i, t in enumerate(stream_targets)
        ]

    def normal_copies(ref, sends, recvs):
        out = []
        for o in range(1, n_normal):
            out.append(pltpu.make_async_remote_copy(
                src_ref=ref.at[me], dst_ref=ref.at[me], send_sem=sends.at[o - 1], recv_sem=recvs.at[o - 1],
                device_id={"normal": lax.rem(me + o, n_normal)}, device_id_type=MESH))
        return out

    def normal_arrivals(ref, sends, recvs):
        out = []
        for o in range(1, n_normal):
            came = lax.rem(me + n_normal - o, n_normal)
            out.append(pltpu.make_async_remote_copy(
                src_ref=ref.at[me], dst_ref=ref.at[came], send_sem=sends.at[o - 1], recv_sem=recvs.at[o - 1],
                device_id={"normal": lax.rem(me + o, n_normal)}, device_id_type=MESH))
        return out

    lane = lax.broadcasted_iota(jnp.int32, (K, LANES), 1)
    chunk = lax.broadcasted_iota(jnp.int32, (K, LANES), 0)

    def vec_rows(ref, j):
        return [ref[pl.ds(j * N + c, K, stride=J * N), :] for c in range(N)]

    def mat_rows(ref, j, first=0):
        return [[ref[pl.ds(first + j * N * N + c * N + e, K, stride=J * N * N), :] for e in range(N)] for c in range(N)]

    def get_mat(ref, *at):
        return [[ref[(*at, c, e)] for e in range(N)] for c in range(N)]

    def put_mat(ref, mat, *at):
        for c in range(N):
            for e in range(N):
                ref[(*at, c, e)] = mat[c][e]

    def x_rows(sweep, j):
        if sweep == 0:
            return vec_rows(xb, j)
        return [xk[sweep - 1, j * N + c] for c in range(N)]

    def send_edges(sweep):
        packed = jnp.zeros((K, LANES), jnp.float32)
        for j in range(J):
            rows = x_rows(sweep, j)
            for c in range(N):
                i = j * N + c
                packed = jnp.where(lane >> 1 == i, pltpu.roll(rows[c], 2 * i + 1, 1), packed)
        edge_out[sweep] = packed
        copies = edge_copies(sweep)
        for copy in copies:
            copy.start()
        return copies

    span_now = span_copies()
    for copy in span_now:
        copy.start()
    ld_x.wait()
    edge_now = send_edges(0)
    pending = list(span_now) + list(edge_now)

    ld_low.wait()
    ld_upp.wait()

    first = mat_map(lambda a: -a, mat_rows(low, 0))
    put_mat(fw, first, 0)

    def fw_step(j, carry):
        carry = mat_mat(mat_map(lambda a: -a, mat_rows(low, j)), carry)
        put_mat(fw, carry, j)
        return carry

    last_f = lax.fori_loop(1, J, fw_step, first)
    start_b = mat_map(lambda a: -a, mat_rows(upp, J - 1))
    put_mat(bw, start_b, J - 1)
    put_mat(gw, last_f, J - 1)

    def bw_step(i, carry):
        j = J - 2 - i
        carry = mat_mat(mat_map(lambda a: -a, mat_rows(upp, j)), carry)
        put_mat(bw, carry, j)
        return carry

    def gw_step(i, carry):
        j = J - 2 - i
        moved = mat_mat(mat_rows(upp, j), carry)
        carry = mat_map(lambda a, b: a - b, get_mat(fw, j), moved)
        put_mat(gw, carry, j)
        return carry

    first_b = lax.fori_loop(0, J - 1, bw_step, start_b)
    first_g = lax.fori_loop(0, J - 1, gw_step, last_f)

    steps = (1, 2, 4)
    whole = last_f
    for level, s in enumerate(steps):
        put_mat(scan_f, mat_map(lambda a: jnp.where(chunk >= s, a, 0.0), whole), level)
        moved = mat_mat(whole, mat_map(lambda a: pltpu.roll(a, s, 0), whole))
        whole = mat_map(lambda a, b: jnp.where(chunk >= s, b, a), whole, moved)
    before = mat_map(lambda a: pltpu.roll(a, 1, 0), whole)
    before = [[jnp.where(chunk >= 1, before[c][e], 1.0 if c == e else 0.0) for e in range(N)] for c in range(N)]
    put_mat(excl, before, 0)
    for c in range(N):
        for e in range(N):
            map_all[me, pl.ds(c * N + e, 1), :] = whole[c][e][K - 1:K]
    seen = mat_mat(first_g, before)
    put_mat(excl, seen, 1)

    whole = first_b
    for level, s in enumerate(steps):
        put_mat(scan_b, mat_map(lambda a: jnp.where(chunk < K - s, a, 0.0), whole), level)
        moved = mat_mat(whole, mat_map(lambda a: pltpu.roll(a, K - s, 0), whole))
        whole = mat_map(lambda a, b: jnp.where(chunk < K - s, b, a), whole, moved)
    after = mat_map(lambda a: pltpu.roll(a, K - 1, 0), whole)
    after = [[jnp.where(chunk < K - 1, after[c][e], 1.0 if c == e else 0.0) for e in range(N)] for c in range(N)]
    put_mat(excl, after, 2)
    for c in range(N):
        for e in range(N):
            map_all[me, pl.ds(N * N + c * N + e, 1), :] = whole[c][e][0:1]
    seen = get_mat(excl, 1)
    for level, s in enumerate(steps):
        moved = mat_mat(get_mat(scan_b, level), mat_map(lambda a: pltpu.roll(a, K - s, 0), seen))
        seen = mat_map(jnp.add, seen, moved)
    for c in range(N):
        for e in range(N):
            map_all[me, pl.ds(2 * N * N + c * N + e, 1), :] = seen[c][e][0:1]
    put_mat(excl, mat_map(lambda a: jnp.where(chunk < K - 1, pltpu.roll(a, K - 1, 0), 0.0), seen), 1)
    map_now = normal_copies(map_all, map_send, map_recv)
    for copy in map_now:
        copy.start()
    pending += map_now

    for sweep in range(SWEEPS):
        if sweep == 0:
            ld_don.wait()
        places = [don[pl.ds(j, K, stride=J), :] for j in range(J)]
        row_of = [p >> 7 for p in places]
        col_of = [p & (LANES - 1) for p in places]

        def gather_step(jj, carry):
            carry = list(carry)
            for k in range(K):
                if sweep == 0:
                    ones = [xb[pl.ds((k * J + jj) * N + c, 1), :] for c in range(N)]
                else:
                    ones = [xk[sweep - 1, jj * N + c, k:k + 1, :] for c in range(N)]
                rows = [jnp.broadcast_to(one, (K, LANES)) for one in ones]
                for j in range(J):
                    hit = row_of[j] == k * J + jj
                    for c in range(N):
                        got = lane_gather(rows[c], col_of[j])
                        carry[j * N + c] = jnp.where(hit, got, carry[j * N + c])
            return carry

        got = lax.fori_loop(0, J, gather_step, [jnp.zeros((K, LANES), jnp.float32)] * (J * N))
        for i in range(J * N):
            donated[i] = got[i]

        if sweep == 0:
            for load in (ld_src, ld_ibl, ld_cpl):
                load.wait()
        for copy in edge_now:
            copy.wait_recv()
        left = edge_in[sweep, 0]
        right = edge_in[sweep, sides_stream - 1]
        lows, highs = [], []
        for j in range(J):
            rows = x_rows(sweep, j)
            flag = ibl[pl.ds(j, K, stride=J), :]
            lows, highs = [], []
            for c in range(N):
                i = j * N + c
                lows.append(jnp.where(lane == 0, pltpu.roll(left, (LANES - 2 * i) % LANES, 1), pltpu.roll(rows[c], 1, 1)))
                highs.append(jnp.where(lane == LANES - 1, pltpu.roll(right, LANES - 2 - 2 * i, 1), pltpu.roll(rows[c], LANES - 1, 1)))
            c2 = mat_rows(cpl, j, 2 * J * K * N * N)
            c3 = mat_rows(cpl, j, 3 * J * K * N * N)
            s_rows = vec_rows(src, j)
            for c in range(N):
                acc = s_rows[c] + jnp.where(flag == 2, donated[j * N + c], 0.0)
                for e in range(N):
                    acc = acc - (c2[e][c] * lows[e] + c3[e][c] * highs[e])
                base[j * N + c] = acc

        if sweep == 0:
            for copy in span_now:
                copy.wait_recv()
            ld_piv.wait()

        def forward_step(j, state):
            c0 = mat_rows(cpl, j)
            c1 = mat_rows(cpl, j, J * K * N * N)
            flag = ibl[pl.ds(j, K, stride=J), :]
            if sweep == 0:
                sides = [vec_rows(plane.at[i], j) for i in range(sides_span)]
            else:
                sides = [[plane_k[sweep - 1, i, j * N + c] for c in range(N)] for i in range(sides_span)]
            x0 = sides[0]
            rhs = []
            if sides_span == 1:
                both = mat_map(jnp.add, c0, c1)
                for c in range(N):
                    acc = functools.reduce(jnp.add, [both[e][c] * x0[e] for e in range(N)])
                    rhs.append(jnp.where(flag == 0, 0.0, base[j * N + c] - acc))
            else:
                x1 = sides[1]
                for c in range(N):
                    acc = functools.reduce(jnp.add, [c0[e][c] * x0[e] + c1[e][c] * x1[e] for e in range(N)])
                    rhs.append(jnp.where(flag == 0, 0.0, base[j * N + c] - acc))
            scaled = mat_vec(mat_rows(piv, j), rhs)
            moved = mat_vec(mat_rows(low, j), state)
            state = [a - b for a, b in zip(scaled, moved)]
            for c in range(N):
                work[j * N + c] = state[c]
            return state

        zero = [jnp.zeros((K, LANES), jnp.float32)] * N
        f = zero
        for j in range(J):
            if sweep > 0 and j % group == 0:
                for copy in piece_copies(sweep, j // group):
                    copy.wait_recv()
            f = forward_step(j, f)

        def backward_step(i, state):
            j = J - 1 - i
            moved = mat_vec(mat_rows(upp, j), state)
            state = [work[j * N + c] - moved[c] for c in range(N)]
            for c in range(N):
                work[j * N + c] = state[c]
            return state

        b = lax.fori_loop(0, J, backward_step, zero, unroll=True)
        for level, s in enumerate(steps):
            f = vec_add(f, mat_vec(get_mat(scan_f, level), [pltpu.roll(v, s, 0) for v in f]))
        y_in = [jnp.where(chunk >= 1, pltpu.roll(v, 1, 0), 0.0) for v in f]
        b = vec_add(b, mat_vec(get_mat(gw, 0), y_in))
        for level, s in enumerate(steps):
            b = vec_add(b, mat_vec(get_mat(scan_b, level), [pltpu.roll(v, K - s, 0) for v in b]))
        x_in = [jnp.where(chunk < K - 1, pltpu.roll(v, K - 1, 0), 0.0) for v in b]
        for c in range(N):
            vec_all[sweep, me, pl.ds(c, 1), :] = f[c][K - 1:K]
            vec_all[sweep, me, pl.ds(K + c, 1), :] = b[c][0:1]
        sends = normal_copies(vec_all.at[sweep], vec_send.at[sweep], vec_recv.at[sweep])
        for copy in sends:
            copy.start()
        pending += sends
        if sweep == 0:
            for copy in normal_arrivals(map_all, map_send, map_recv):
                copy.wait_recv()
        for copy in normal_arrivals(vec_all.at[sweep], vec_send.at[sweep], vec_recv.at[sweep]):
            copy.wait_recv()

        def apply_map(d, m, state):
            return functools.reduce(jnp.add, [
                map_all[d, pl.ds(m * N * N + e, N, stride=N), :] * state[e:e + 1] for e in range(N)])

        none = jnp.zeros((N, LANES), jnp.float32)
        entries, state, mine = [none], none, none
        for d in range(n_normal - 1):
            state = vec_all[sweep, d, pl.ds(0, N), :] + apply_map(d, 0, state)
            entries.append(state)
            mine = jnp.where(me == d + 1, state, mine)
        x_state, x_mine = none, none
        for d in range(n_normal - 1, 0, -1):
            x_state = (vec_all[sweep, d, pl.ds(K, N), :] + apply_map(d, 2, entries[d])) + apply_map(d, 1, x_state)
            x_mine = jnp.where(me == d - 1, x_state, x_mine)
        y_entry = [jnp.broadcast_to(mine[c:c + 1], (K, LANES)) for c in range(N)]
        x_entry = [jnp.broadcast_to(x_mine[c:c + 1], (K, LANES)) for c in range(N)]
        y_in = vec_add(y_in, mat_vec(get_mat(excl, 0), y_entry))
        x_in = vec_add(x_in, mat_vec(get_mat(excl, 1), y_entry))
        x_in = vec_add(x_in, mat_vec(get_mat(excl, 2), x_entry))

        for j in range(J):
            more = vec_add(mat_vec(get_mat(gw, j), y_in), mat_vec(get_mat(bw, j), x_in))
            for c in range(N):
                value = work[j * N + c] + more[c]
                if sweep == SWEEPS - 1:
                    out_ref[pl.ds(j * N + c, K, stride=J * N), :] = value
                else:
                    xk[sweep, j * N + c] = value
            if sweep < SWEEPS - 1 and j % group == group - 1:
                copies = piece_copies(sweep + 1, j // group)
                for copy in copies:
                    copy.start()
                pending += copies
        if sweep < SWEEPS - 1:
            edge_now = send_edges(sweep + 1)
            pending += edge_now

    for copy in pending:
        copy.wait_send()


def per_device(sizes, iterate, source, pivot, lower, upper, coupling, iblank, donor):
    points, comps, planes, lines = iterate.shape
    n_normal, n_span, n_stream = sizes
    J = points // K
    rows, mats = points * N, points * N * N
    sides_span, sides_stream = (1 if n_span == 2 else 2), (1 if n_stream == 2 else 2)
    f32 = jnp.float32
    peers = max(n_normal - 1, 1)
    scratch = [
        pltpu.VMEM((rows, LANES), f32),
        pltpu.VMEM((SWEEPS - 1, J * N, K, LANES), f32),
        pltpu.VMEM((rows, LANES), f32),
        pltpu.VMEM((mats, LANES), f32),
        pltpu.VMEM((mats, LANES), f32),
        pltpu.VMEM((mats, LANES), f32),
        pltpu.VMEM((4 * mats, LANES), f32),
        pltpu.VMEM((points, LANES), jnp.int32),
        pltpu.VMEM((points, LANES), jnp.int32),
        pltpu.VMEM((sides_span, rows, LANES), f32),
        pltpu.VMEM((SWEEPS - 1, sides_span, J * N, K, LANES), f32),
        pltpu.VMEM((SWEEPS, K, LANES), f32),
        pltpu.VMEM((SWEEPS, sides_stream, K, LANES), f32),
        pltpu.VMEM((SWEEPS, n_normal, 2 * K, LANES), f32),
        pltpu.VMEM((n_normal, 80, LANES), f32),
        pltpu.VMEM((J, N, N, K, LANES), f32),
        pltpu.VMEM((J, N, N, K, LANES), f32),
        pltpu.VMEM((J, N, N, K, LANES), f32),
        pltpu.VMEM((3, N, N, K, LANES), f32),
        pltpu.VMEM((3, N, N, K, LANES), f32),
        pltpu.VMEM((3, N, N, K, LANES), f32),
        pltpu.VMEM((J * N, K, LANES), f32),
        pltpu.VMEM((J * N, K, LANES), f32),
        pltpu.VMEM((J * N, K, LANES), f32),
        pltpu.SemaphoreType.DMA((8,)),
        pltpu.SemaphoreType.DMA((sides_span,)),
        pltpu.SemaphoreType.DMA((sides_span,)),
        pltpu.SemaphoreType.DMA((SWEEPS - 1, J, sides_span)),
        pltpu.SemaphoreType.DMA((SWEEPS - 1, J, sides_span)),
        pltpu.SemaphoreType.DMA((SWEEPS, sides_stream)),
        pltpu.SemaphoreType.DMA((SWEEPS, sides_stream)),
        pltpu.SemaphoreType.DMA((SWEEPS, peers)),
        pltpu.SemaphoreType.DMA((SWEEPS, peers)),
        pltpu.SemaphoreType.DMA((peers,)),
        pltpu.SemaphoreType.DMA((peers,)),
    ]
    out = pl.pallas_call(
        functools.partial(kernel, sizes, J),
        out_shape=pltpu.VMEM((rows, LANES), f32),
        in_specs=[pl.BlockSpec(memory_space=pltpu.HBM)] * 8,
        out_specs=pl.BlockSpec(memory_space=pltpu.VMEM),
        scratch_shapes=scratch,
        compiler_params=pltpu.CompilerParams(
            collective_id=0, has_side_effects=True, vmem_limit_bytes=32 * 1024 * 1024),
        cost_estimate=pl.CostEstimate(flops=12000000, bytes_accessed=5000000, transcendentals=0),
    )(*[
        pltpu.with_memory_space_constraint(operand, pltpu.HBM) for operand in (
            iterate.reshape(rows, lines), source.reshape(rows, lines), pivot.reshape(mats, lines),
            lower.reshape(mats, lines), upper.reshape(mats, lines), coupling.reshape(4 * mats, lines),
            iblank.reshape(points, lines), donor.reshape(points, lines))
    ])
    return out.reshape(points, comps, planes, lines)


def solution(mesh):
    placed = (
        P("normal", None, "span", "stream"),
        P("normal", None, "span", "stream"),
        P("normal", None, None, "span", "stream"),
        P("normal", None, None, "span", "stream"),
        P("normal", None, None, "span", "stream"),
        P(None, "normal", None, None, "span", "stream"),
        P("normal", "span", "stream"),
        P("normal", "span", "stream"),
    )
    sizes = tuple(mesh.shape[name] for name in ("normal", "span", "stream"))
    return jax.shard_map(
        functools.partial(per_device, sizes),
        mesh=mesh,
        in_specs=placed,
        out_specs=P("normal", None, "span", "stream"),
        check_vma=False,
    )
```

```python
import functools
import jax
import jax.numpy as jnp
from jax import lax
from jax.experimental import pallas as pl
from jax.experimental.pallas import tpu as pltpu
from jax.sharding import PartitionSpec as P

SWEEPS = 2
N = 5
K = 8
LANES = 128
MESH = pl.DeviceIdType.MESH


def tree_sum(terms):
    while len(terms) > 1:
        terms = [a + b for a, b in zip(terms[::2], terms[1::2])] + ([terms[-1]] if len(terms) % 2 else [])
    return terms[0]


def mat_vec(mat, vec):
    return [tree_sum([mat[c][e] * vec[e] for e in range(N)]) for c in range(N)]


def mat_mat(left, right):
    return [
        [tree_sum([left[c][e] * right[e][f] for e in range(N)]) for f in range(N)]
        for c in range(N)
    ]


def mat_map(function, *mats):
    return [[function(*(m[c][e] for m in mats)) for e in range(N)] for c in range(N)]


def vec_add(a, b):
    return [p + q for p, q in zip(a, b)]


def lane_gather(row, index):
    numbers = lax.GatherDimensionNumbers(
        offset_dims=(), collapsed_slice_dims=(1,), start_index_map=(1,),
        operand_batching_dims=(0,), start_indices_batching_dims=(0,))
    return lax.gather(row, index[..., None], numbers, (1, 1), mode=lax.GatherScatterMode.PROMISE_IN_BOUNDS)


def kernel(sizes, per_chunk, x_hbm, src_hbm, piv_hbm, low_hbm, upp_hbm, cpl_hbm, ibl_hbm, don_hbm, out_ref,
           xb, xk, src, piv, low, upp, cpl, ibl, don, plane, plane_k, edge_out, edge_in, vec_all, map_all,
           fw, gw, bw, scan_f, scan_b, excl, base, work, donated,
           load_sem, span_send, span_recv, piece_send, piece_recv, edge_send, edge_recv, vec_send, vec_recv, map_send, map_recv):
    J = per_chunk
    n_normal, n_span, n_stream = sizes
    me, sp, st = lax.axis_index("normal"), lax.axis_index("span"), lax.axis_index("stream")
    span_targets = [lax.rem(sp + 1, n_span)] if n_span == 2 else [lax.rem(sp + 1, n_span), lax.rem(sp + n_span - 1, n_span)]
    stream_targets = [lax.rem(st + 1, n_stream)] if n_stream == 2 else [lax.rem(st + 1, n_stream), lax.rem(st + n_stream - 1, n_stream)]
    sides_span, sides_stream = len(span_targets), len(stream_targets)

    pairs = [(x_hbm, xb), (low_hbm, low), (upp_hbm, upp), (don_hbm, don), (cpl_hbm, cpl),
             (src_hbm, src), (ibl_hbm, ibl), (piv_hbm, piv)]
    loads = [pltpu.make_async_copy(a, b, load_sem.at[i]) for i, (a, b) in enumerate(pairs)]
    for load in loads:
        load.start()
    ld_x, ld_low, ld_upp, ld_don, ld_cpl, ld_src, ld_ibl, ld_piv = loads

    barrier = pltpu.get_barrier_semaphore()
    for t in span_targets:
        pl.semaphore_signal(barrier, inc=1, device_id={"span": t}, device_id_type=MESH)
    for t in stream_targets:
        pl.semaphore_signal(barrier, inc=1, device_id={"stream": t}, device_id_type=MESH)
    for o in range(1, n_normal):
        pl.semaphore_signal(barrier, inc=1, device_id={"normal": lax.rem(me + o, n_normal)}, device_id_type=MESH)
    pl.semaphore_wait(barrier, sides_span + sides_stream + n_normal - 1)

    def span_copies():
        return [
            pltpu.make_async_remote_copy(
                src_ref=x_hbm, dst_ref=plane.at[i], send_sem=span_send.at[i],
                recv_sem=span_recv.at[i], device_id={"span": t}, device_id_type=MESH)
            for i, t in enumerate(span_targets)
        ]

    group = 2 if J % 2 == 0 else 1

    def piece_copies(sweep, piece):
        part = pl.ds(piece * group * N, group * N)
        return [
            pltpu.make_async_remote_copy(
                src_ref=xk.at[sweep - 1, part], dst_ref=plane_k.at[sweep - 1, i, part],
                send_sem=piece_send.at[sweep - 1, piece, i], recv_sem=piece_recv.at[sweep - 1, piece, i],
                device_id={"span": t}, device_id_type=MESH)
            for i, t in enumerate(span_targets)
        ]

    def edge_copies(sweep):
        return [
            pltpu.make_async_remote_copy(
                src_ref=edge_out.at[sweep], dst_ref=edge_in.at[sweep, i], send_sem=edge_send.at[sweep, i],
                recv_sem=edge_recv.at[sweep, i], device_id={"stream": t}, device_id_type=MESH)
            for i, t in enumerate(stream_targets)
        ]

    def normal_copies(ref, sends, recvs):
        out = []
        for o in range(1, n_normal):
            out.append(pltpu.make_async_remote_copy(
                src_ref=ref.at[me], dst_ref=ref.at[me], send_sem=sends.at[o - 1], recv_sem=recvs.at[o - 1],
                device_id={"normal": lax.rem(me + o, n_normal)}, device_id_type=MESH))
        return out

    def normal_arrivals(ref, sends, recvs):
        out = []
        for o in range(1, n_normal):
            came = lax.rem(me + n_normal - o, n_normal)
            out.append(pltpu.make_async_remote_copy(
                src_ref=ref.at[me], dst_ref=ref.at[came], send_sem=sends.at[o - 1], recv_sem=recvs.at[o - 1],
                device_id={"normal": lax.rem(me + o, n_normal)}, device_id_type=MESH))
        return out

    lane = lax.broadcasted_iota(jnp.int32, (K, LANES), 1)
    chunk = lax.broadcasted_iota(jnp.int32, (K, LANES), 0)

    def vec_rows(ref, j):
        return [ref[pl.ds(j * N + c, K, stride=J * N), :] for c in range(N)]

    def mat_rows(ref, j, first=0):
        return [[ref[pl.ds(first + j * N * N + c * N + e, K, stride=J * N * N), :] for e in range(N)] for c in range(N)]

    def get_mat(ref, *at):
        return [[ref[(*at, c, e)] for e in range(N)] for c in range(N)]

    def put_mat(ref, mat, *at):
        for c in range(N):
            for e in range(N):
                ref[(*at, c, e)] = mat[c][e]

    def x_rows(sweep, j):
        if sweep == 0:
            return vec_rows(xb, j)
        return [xk[sweep - 1, j * N + c] for c in range(N)]

    def send_edges(sweep):
        packed = jnp.zeros((K, LANES), jnp.float32)
        for j in range(J):
            rows = x_rows(sweep, j)
            for c in range(N):
                i = j * N + c
                packed = jnp.where(lane >> 1 == i, pltpu.roll(rows[c], 2 * i + 1, 1), packed)
        edge_out[sweep] = packed
        copies = edge_copies(sweep)
        for copy in copies:
            copy.start()
        return copies

    span_now = span_copies()
    for copy in span_now:
        copy.start()
    ld_x.wait()
    edge_now = send_edges(0)
    pending = list(span_now) + list(edge_now)

    def gather_donors(sweep):
        places = [don[pl.ds(j, K, stride=J), :] for j in range(J)]
        row_of = [p >> 7 for p in places]
        col_of = [p & (LANES - 1) for p in places]

        def gather_step(jj, carry):
            carry = list(carry)
            for k in range(K):
                if sweep == 0:
                    ones = [xb[pl.ds((k * J + jj) * N + c, 1), :] for c in range(N)]
                else:
                    ones = [xk[sweep - 1, jj * N + c, k:k + 1, :] for c in range(N)]
                rows = [jnp.broadcast_to(one, (K, LANES)) for one in ones]
                for j in range(J):
                    hit = row_of[j] == k * J + jj
                    for c in range(N):
                        got = lane_gather(rows[c], col_of[j])
                        carry[j * N + c] = jnp.where(hit, got, carry[j * N + c])
            return carry

        got = lax.fori_loop(0, J, gather_step, [jnp.zeros((K, LANES), jnp.float32)] * (J * N))
        for i in range(J * N):
            donated[i] = got[i]

    ld_don.wait()
    gather_donors(0)
    ld_low.wait()
    ld_upp.wait()

    first = mat_map(lambda a: -a, mat_rows(low, 0))
    put_mat(fw, first, 0)

    def fw_step(j, carry):
        carry = mat_mat(mat_map(lambda a: -a, mat_rows(low, j)), carry)
        put_mat(fw, carry, j)
        return carry

    last_f = lax.fori_loop(1, J, fw_step, first)
    start_b = mat_map(lambda a: -a, mat_rows(upp, J - 1))
    put_mat(bw, start_b, J - 1)
    put_mat(gw, last_f, J - 1)

    def back_step(i, carry):
        j = J - 2 - i
        block = mat_rows(upp, j)
        b_now = mat_map(lambda a: -a, mat_mat(block, carry[0]))
        g_now = mat_map(lambda a, b: a - b, get_mat(fw, j), mat_mat(block, carry[1]))
        put_mat(bw, b_now, j)
        put_mat(gw, g_now, j)
        return b_now, g_now

    first_b, first_g = lax.fori_loop(0, J - 1, back_step, (start_b, last_f))

    steps = (1, 2, 4)
    whole = last_f
    for level, s in enumerate(steps):
        put_mat(scan_f, mat_map(lambda a: jnp.where(chunk >= s, a, 0.0), whole), level)
        moved = mat_mat(whole, mat_map(lambda a: pltpu.roll(a, s, 0), whole))
        whole = mat_map(lambda a, b: jnp.where(chunk >= s, b, a), whole, moved)
    before = mat_map(lambda a: pltpu.roll(a, 1, 0), whole)
    before = [[jnp.where(chunk >= 1, before[c][e], 1.0 if c == e else 0.0) for e in range(N)] for c in range(N)]
    put_mat(excl, before, 0)
    for c in range(N):
        for e in range(N):
            map_all[me, pl.ds(c * N + e, 1), :] = whole[c][e][K - 1:K]
    seen = mat_mat(first_g, before)
    put_mat(excl, seen, 1)

    whole = first_b
    for level, s in enumerate(steps):
        put_mat(scan_b, mat_map(lambda a: jnp.where(chunk < K - s, a, 0.0), whole), level)
        moved = mat_mat(whole, mat_map(lambda a: pltpu.roll(a, K - s, 0), whole))
        whole = mat_map(lambda a, b: jnp.where(chunk < K - s, b, a), whole, moved)
    after = mat_map(lambda a: pltpu.roll(a, K - 1, 0), whole)
    after = [[jnp.where(chunk < K - 1, after[c][e], 1.0 if c == e else 0.0) for e in range(N)] for c in range(N)]
    put_mat(excl, after, 2)
    for c in range(N):
        for e in range(N):
            map_all[me, pl.ds(N * N + c * N + e, 1), :] = whole[c][e][0:1]
    seen = get_mat(excl, 1)
    for level, s in enumerate(steps):
        moved = mat_mat(get_mat(scan_b, level), mat_map(lambda a: pltpu.roll(a, K - s, 0), seen))
        seen = mat_map(jnp.add, seen, moved)
    for c in range(N):
        for e in range(N):
            map_all[me, pl.ds(2 * N * N + c * N + e, 1), :] = seen[c][e][0:1]
    put_mat(excl, mat_map(lambda a: jnp.where(chunk < K - 1, pltpu.roll(a, K - 1, 0), 0.0), seen), 1)
    map_now = normal_copies(map_all, map_send, map_recv)
    for copy in map_now:
        copy.start()
    pending += map_now

    for sweep in range(SWEEPS):
        if sweep > 0:
            gather_donors(sweep)
        if sweep == 0:
            for load in (ld_src, ld_ibl, ld_cpl):
                load.wait()
        for copy in edge_now:
            copy.wait_recv()
        left = edge_in[sweep, 0]
        right = edge_in[sweep, sides_stream - 1]
        lows, highs = [], []
        for j in range(J):
            rows = x_rows(sweep, j)
            flag = ibl[pl.ds(j, K, stride=J), :]
            lows, highs = [], []
            for c in range(N):
                i = j * N + c
                lows.append(jnp.where(lane == 0, pltpu.roll(left, (LANES - 2 * i) % LANES, 1), pltpu.roll(rows[c], 1, 1)))
                highs.append(jnp.where(lane == LANES - 1, pltpu.roll(right, LANES - 2 - 2 * i, 1), pltpu.roll(rows[c], LANES - 1, 1)))
            c2 = mat_rows(cpl, j, 2 * J * K * N * N)
            c3 = mat_rows(cpl, j, 3 * J * K * N * N)
            s_rows = vec_rows(src, j)
            for c in range(N):
                acc = s_rows[c] + jnp.where(flag == 2, donated[j * N + c], 0.0)
                for e in range(N):
                    acc = acc - (c2[e][c] * lows[e] + c3[e][c] * highs[e])
                base[j * N + c] = acc

        if sweep == 0:
            for copy in span_now:
                copy.wait_recv()
            ld_piv.wait()

        def forward_step(j, state):
            c0 = mat_rows(cpl, j)
            c1 = mat_rows(cpl, j, J * K * N * N)
            flag = ibl[pl.ds(j, K, stride=J), :]
            if sweep == 0:
                sides = [vec_rows(plane.at[i], j) for i in range(sides_span)]
            else:
                sides = [[plane_k[sweep - 1, i, j * N + c] for c in range(N)] for i in range(sides_span)]
            x0 = sides[0]
            rhs = []
            if sides_span == 1:
                both = mat_map(jnp.add, c0, c1)
                for c in range(N):
                    acc = tree_sum([both[e][c] * x0[e] for e in range(N)])
                    rhs.append(jnp.where(flag == 0, 0.0, base[j * N + c] - acc))
            else:
                x1 = sides[1]
                for c in range(N):
                    acc = tree_sum([c0[e][c] * x0[e] + c1[e][c] * x1[e] for e in range(N)])
                    rhs.append(jnp.where(flag == 0, 0.0, base[j * N + c] - acc))
            scaled = mat_vec(mat_rows(piv, j), rhs)
            moved = mat_vec(mat_rows(low, j), state)
            state = [a - b for a, b in zip(scaled, moved)]
            for c in range(N):
                work[j * N + c] = state[c]
            return state

        zero = [jnp.zeros((K, LANES), jnp.float32)] * N
        f = zero
        for j in range(J):
            if sweep > 0 and j % group == 0:
                for copy in piece_copies(sweep, j // group):
                    copy.wait_recv()
            f = forward_step(j, f)

        def backward_step(i, state):
            j = J - 1 - i
            moved = mat_vec(mat_rows(upp, j), state)
            state = [work[j * N + c] - moved[c] for c in range(N)]
            for c in range(N):
                work[j * N + c] = state[c]
            return state

        b = lax.fori_loop(0, J, backward_step, zero, unroll=True)
        for level, s in enumerate(steps):
            f = vec_add(f, mat_vec(get_mat(scan_f, level), [pltpu.roll(v, s, 0) for v in f]))
        y_in = [jnp.where(chunk >= 1, pltpu.roll(v, 1, 0), 0.0) for v in f]
        b = vec_add(b, mat_vec(get_mat(gw, 0), y_in))
        for level, s in enumerate(steps):
            b = vec_add(b, mat_vec(get_mat(scan_b, level), [pltpu.roll(v, K - s, 0) for v in b]))
        x_in = [jnp.where(chunk < K - 1, pltpu.roll(v, K - 1, 0), 0.0) for v in b]
        for c in range(N):
            vec_all[sweep, me, pl.ds(c, 1), :] = f[c][K - 1:K]
            vec_all[sweep, me, pl.ds(K + c, 1), :] = b[c][0:1]
        sends = normal_copies(vec_all.at[sweep], vec_send.at[sweep], vec_recv.at[sweep])
        for copy in sends:
            copy.start()
        pending += sends
        if sweep == 0:
            for copy in normal_arrivals(map_all, map_send, map_recv):
                copy.wait_recv()
        for copy in normal_arrivals(vec_all.at[sweep], vec_send.at[sweep], vec_recv.at[sweep]):
            copy.wait_recv()

        def apply_map(d, m, state):
            return tree_sum([
                map_all[d, pl.ds(m * N * N + e, N, stride=N), :] * state[e:e + 1] for e in range(N)])

        none = jnp.zeros((N, LANES), jnp.float32)
        entries, state, mine = [none], none, none
        for d in range(n_normal - 1):
            state = vec_all[sweep, d, pl.ds(0, N), :] + apply_map(d, 0, state)
            entries.append(state)
            mine = jnp.where(me == d + 1, state, mine)
        x_state, x_mine = none, none
        for d in range(n_normal - 1, 0, -1):
            x_state = (vec_all[sweep, d, pl.ds(K, N), :] + apply_map(d, 2, entries[d])) + apply_map(d, 1, x_state)
            x_mine = jnp.where(me == d - 1, x_state, x_mine)
        y_entry = [jnp.broadcast_to(mine[c:c + 1], (K, LANES)) for c in range(N)]
        x_entry = [jnp.broadcast_to(x_mine[c:c + 1], (K, LANES)) for c in range(N)]
        y_in = vec_add(y_in, mat_vec(get_mat(excl, 0), y_entry))
        x_in = vec_add(x_in, mat_vec(get_mat(excl, 1), y_entry))
        x_in = vec_add(x_in, mat_vec(get_mat(excl, 2), x_entry))

        for j in range(J):
            more = vec_add(mat_vec(get_mat(gw, j), y_in), mat_vec(get_mat(bw, j), x_in))
            for c in range(N):
                value = work[j * N + c] + more[c]
                if sweep == SWEEPS - 1:
                    out_ref[pl.ds(j * N + c, K, stride=J * N), :] = value
                else:
                    xk[sweep, j * N + c] = value
            if sweep < SWEEPS - 1 and j % group == group - 1:
                copies = piece_copies(sweep + 1, j // group)
                for copy in copies:
                    copy.start()
                pending += copies
        if sweep < SWEEPS - 1:
            edge_now = send_edges(sweep + 1)
            pending += edge_now

    for copy in pending:
        copy.wait_send()


def per_device(sizes, iterate, source, pivot, lower, upper, coupling, iblank, donor):
    points, comps, planes, lines = iterate.shape
    n_normal, n_span, n_stream = sizes
    J = points // K
    rows, mats = points * N, points * N * N
    sides_span, sides_stream = (1 if n_span == 2 else 2), (1 if n_stream == 2 else 2)
    f32 = jnp.float32
    peers = max(n_normal - 1, 1)
    scratch = [
        pltpu.VMEM((rows, LANES), f32),
        pltpu.VMEM((SWEEPS - 1, J * N, K, LANES), f32),
        pltpu.VMEM((rows, LANES), f32),
        pltpu.VMEM((mats, LANES), f32),
        pltpu.VMEM((mats, LANES), f32),
        pltpu.VMEM((mats, LANES), f32),
        pltpu.VMEM((4 * mats, LANES), f32),
        pltpu.VMEM((points, LANES), jnp.int32),
        pltpu.VMEM((points, LANES), jnp.int32),
        pltpu.VMEM((sides_span, rows, LANES), f32),
        pltpu.VMEM((SWEEPS - 1, sides_span, J * N, K, LANES), f32),
        pltpu.VMEM((SWEEPS, K, LANES), f32),
        pltpu.VMEM((SWEEPS, sides_stream, K, LANES), f32),
        pltpu.VMEM((SWEEPS, n_normal, 2 * K, LANES), f32),
        pltpu.VMEM((n_normal, 80, LANES), f32),
        pltpu.VMEM((J, N, N, K, LANES), f32),
        pltpu.VMEM((J, N, N, K, LANES), f32),
        pltpu.VMEM((J, N, N, K, LANES), f32),
        pltpu.VMEM((3, N, N, K, LANES), f32),
        pltpu.VMEM((3, N, N, K, LANES), f32),
        pltpu.VMEM((3, N, N, K, LANES), f32),
        pltpu.VMEM((J * N, K, LANES), f32),
        pltpu.VMEM((J * N, K, LANES), f32),
        pltpu.VMEM((J * N, K, LANES), f32),
        pltpu.SemaphoreType.DMA((8,)),
        pltpu.SemaphoreType.DMA((sides_span,)),
        pltpu.SemaphoreType.DMA((sides_span,)),
        pltpu.SemaphoreType.DMA((SWEEPS - 1, J, sides_span)),
        pltpu.SemaphoreType.DMA((SWEEPS - 1, J, sides_span)),
        pltpu.SemaphoreType.DMA((SWEEPS, sides_stream)),
        pltpu.SemaphoreType.DMA((SWEEPS, sides_stream)),
        pltpu.SemaphoreType.DMA((SWEEPS, peers)),
        pltpu.SemaphoreType.DMA((SWEEPS, peers)),
        pltpu.SemaphoreType.DMA((peers,)),
        pltpu.SemaphoreType.DMA((peers,)),
    ]
    out = pl.pallas_call(
        functools.partial(kernel, sizes, J),
        out_shape=pltpu.VMEM((rows, LANES), f32),
        in_specs=[pl.BlockSpec(memory_space=pltpu.HBM)] * 8,
        out_specs=pl.BlockSpec(memory_space=pltpu.VMEM),
        scratch_shapes=scratch,
        compiler_params=pltpu.CompilerParams(
            collective_id=0, has_side_effects=True, vmem_limit_bytes=32 * 1024 * 1024),
        cost_estimate=pl.CostEstimate(flops=12000000, bytes_accessed=5000000, transcendentals=0),
    )(*[
        pltpu.with_memory_space_constraint(operand, pltpu.HBM) for operand in (
            iterate.reshape(rows, lines), source.reshape(rows, lines), pivot.reshape(mats, lines),
            lower.reshape(mats, lines), upper.reshape(mats, lines), coupling.reshape(4 * mats, lines),
            iblank.reshape(points, lines), donor.reshape(points, lines))
    ])
    return out.reshape(points, comps, planes, lines)


def solution(mesh):
    placed = (
        P("normal", None, "span", "stream"),
        P("normal", None, "span", "stream"),
        P("normal", None, None, "span", "stream"),
        P("normal", None, None, "span", "stream"),
        P("normal", None, None, "span", "stream"),
        P(None, "normal", None, None, "span", "stream"),
        P("normal", "span", "stream"),
        P("normal", "span", "stream"),
    )
    sizes = tuple(mesh.shape[name] for name in ("normal", "span", "stream"))
    return jax.shard_map(
        functools.partial(per_device, sizes),
        mesh=mesh,
        in_specs=placed,
        out_specs=P("normal", None, "span", "stream"),
        check_vma=False,
    )
```

```python
import functools
import jax
import jax.numpy as jnp
from jax import lax
from jax.experimental import pallas as pl
from jax.experimental.pallas import tpu as pltpu
from jax.sharding import PartitionSpec as P

SWEEPS = 2
N = 5
K = 8
LANES = 128
MESH = pl.DeviceIdType.MESH


def tree_sum(terms):
    while len(terms) > 1:
        terms = [a + b for a, b in zip(terms[::2], terms[1::2])] + ([terms[-1]] if len(terms) % 2 else [])
    return terms[0]


def mat_vec(mat, vec):
    return [tree_sum([mat[c][e] * vec[e] for e in range(N)]) for c in range(N)]


def mat_mat(left, right):
    return [
        [functools.reduce(jnp.add, [left[c][e] * right[e][f] for e in range(N)]) for f in range(N)]
        for c in range(N)
    ]


def mat_map(function, *mats):
    return [[function(*(m[c][e] for m in mats)) for e in range(N)] for c in range(N)]


def vec_add(a, b):
    return [p + q for p, q in zip(a, b)]


def lane_gather(row, index):
    numbers = lax.GatherDimensionNumbers(
        offset_dims=(), collapsed_slice_dims=(1,), start_index_map=(1,),
        operand_batching_dims=(0,), start_indices_batching_dims=(0,))
    return lax.gather(row, index[..., None], numbers, (1, 1), mode=lax.GatherScatterMode.PROMISE_IN_BOUNDS)


def kernel(sizes, per_chunk, x_hbm, src_hbm, piv_hbm, low_hbm, upp_hbm, cpl_hbm, ibl_hbm, don_hbm, out_ref,
           xb, xk, src, piv, low, upp, cpl, ibl, don, plane, plane_k, edge_out, edge_in, vec_all, map_all,
           fw, gw, bw, scan_f, scan_b, excl, base, work, donated,
           load_sem, span_send, span_recv, piece_send, piece_recv, edge_send, edge_recv, vec_send, vec_recv, map_send, map_recv):
    J = per_chunk
    n_normal, n_span, n_stream = sizes
    me, sp, st = lax.axis_index("normal"), lax.axis_index("span"), lax.axis_index("stream")
    span_targets = [lax.rem(sp + 1, n_span)] if n_span == 2 else [lax.rem(sp + 1, n_span), lax.rem(sp + n_span - 1, n_span)]
    stream_targets = [lax.rem(st + 1, n_stream)] if n_stream == 2 else [lax.rem(st + 1, n_stream), lax.rem(st + n_stream - 1, n_stream)]
    sides_span, sides_stream = len(span_targets), len(stream_targets)

    pairs = [(x_hbm, xb), (low_hbm, low), (upp_hbm, upp), (don_hbm, don), (cpl_hbm, cpl),
             (src_hbm, src), (ibl_hbm, ibl), (piv_hbm, piv)]
    loads = [pltpu.make_async_copy(a, b, load_sem.at[i]) for i, (a, b) in enumerate(pairs)]
    for load in loads:
        load.start()
    ld_x, ld_low, ld_upp, ld_don, ld_cpl, ld_src, ld_ibl, ld_piv = loads

    barrier = pltpu.get_barrier_semaphore()
    for t in span_targets:
        pl.semaphore_signal(barrier, inc=1, device_id={"span": t}, device_id_type=MESH)
    for t in stream_targets:
        pl.semaphore_signal(barrier, inc=1, device_id={"stream": t}, device_id_type=MESH)
    for o in range(1, n_normal):
        pl.semaphore_signal(barrier, inc=1, device_id={"normal": lax.rem(me + o, n_normal)}, device_id_type=MESH)
    pl.semaphore_wait(barrier, sides_span + sides_stream + n_normal - 1)

    def span_copies():
        return [
            pltpu.make_async_remote_copy(
                src_ref=x_hbm, dst_ref=plane.at[i], send_sem=span_send.at[i],
                recv_sem=span_recv.at[i], device_id={"span": t}, device_id_type=MESH)
            for i, t in enumerate(span_targets)
        ]

    group = 2 if J % 2 == 0 else 1

    def piece_copies(sweep, piece):
        part = pl.ds(piece * group * N, group * N)
        return [
            pltpu.make_async_remote_copy(
                src_ref=xk.at[sweep - 1, part], dst_ref=plane_k.at[sweep - 1, i, part],
                send_sem=piece_send.at[sweep - 1, piece, i], recv_sem=piece_recv.at[sweep - 1, piece, i],
                device_id={"span": t}, device_id_type=MESH)
            for i, t in enumerate(span_targets)
        ]

    def edge_copies(sweep):
        return [
            pltpu.make_async_remote_copy(
                src_ref=edge_out.at[sweep], dst_ref=edge_in.at[sweep, i], send_sem=edge_send.at[sweep, i],
                recv_sem=edge_recv.at[sweep, i], device_id={"stream": t}, device_id_type=MESH)
            for i, t in enumerate(stream_targets)
        ]

    def normal_copies(ref, sends, recvs):
        out = []
        for o in range(1, n_normal):
            out.append(pltpu.make_async_remote_copy(
                src_ref=ref.at[me], dst_ref=ref.at[me], send_sem=sends.at[o - 1], recv_sem=recvs.at[o - 1],
                device_id={"normal": lax.rem(me + o, n_normal)}, device_id_type=MESH))
        return out

    def normal_arrivals(ref, sends, recvs):
        out = []
        for o in range(1, n_normal):
            came = lax.rem(me + n_normal - o, n_normal)
            out.append(pltpu.make_async_remote_copy(
                src_ref=ref.at[me], dst_ref=ref.at[came], send_sem=sends.at[o - 1], recv_sem=recvs.at[o - 1],
                device_id={"normal": lax.rem(me + o, n_normal)}, device_id_type=MESH))
        return out

    def map_copies(part, arriving):
        out = []
        for o in range(1, n_normal):
            slot = lax.rem(me + n_normal - o, n_normal) if arriving else me
            copy = pltpu.make_async_remote_copy(
                src_ref=map_all.at[part, me], dst_ref=map_all.at[part, slot],
                send_sem=map_send.at[part, o - 1], recv_sem=map_recv.at[part, o - 1],
                device_id={"normal": lax.rem(me + o, n_normal)}, device_id_type=MESH)
            if part == 0:
                used = slot < n_normal - 1
            else:
                used = me - o < 0 if arriving else me + o >= n_normal
            out.append((used, copy))
        return out

    def send_map(part, mat, row):
        for c in range(N):
            for e in range(N):
                map_all[part, me, pl.ds(c * N + e, 1), :] = mat[c][e][row:row + 1]
        for used, copy in map_copies(part, False):
            @pl.when(used)
            def _(copy=copy):
                copy.start()

    lane = lax.broadcasted_iota(jnp.int32, (K, LANES), 1)
    chunk = lax.broadcasted_iota(jnp.int32, (K, LANES), 0)

    def vec_rows(ref, j):
        return [ref[pl.ds(j * N + c, K, stride=J * N), :] for c in range(N)]

    def mat_rows(ref, j, first=0):
        return [[ref[pl.ds(first + j * N * N + c * N + e, K, stride=J * N * N), :] for e in range(N)] for c in range(N)]

    def get_mat(ref, *at):
        return [[ref[(*at, c, e)] for e in range(N)] for c in range(N)]

    def put_mat(ref, mat, *at):
        for c in range(N):
            for e in range(N):
                ref[(*at, c, e)] = mat[c][e]

    def x_rows(sweep, j):
        if sweep == 0:
            return vec_rows(xb, j)
        return [xk[sweep - 1, j * N + c] for c in range(N)]

    def send_edges(sweep):
        packed = jnp.zeros((K, LANES), jnp.float32)
        for j in range(J):
            rows = x_rows(sweep, j)
            for c in range(N):
                i = j * N + c
                packed = jnp.where(lane >> 1 == i, pltpu.roll(rows[c], 2 * i + 1, 1), packed)
        edge_out[sweep] = packed
        copies = edge_copies(sweep)
        for copy in copies:
            copy.start()
        return copies

    span_now = span_copies()
    for copy in span_now:
        copy.start()
    ld_x.wait()
    edge_now = send_edges(0)
    pending = list(span_now) + list(edge_now)

    for part in (1, 2):
        for d in range(n_normal - 1):
            @pl.when(d < me)
            def _(part=part, d=d):
                map_all[part, d] = jnp.zeros((N * N, LANES), jnp.float32)

    ld_low.wait()

    first = mat_map(lambda a: -a, mat_rows(low, 0))
    put_mat(fw, first, 0)

    def fw_step(j, carry):
        carry = mat_mat(mat_map(lambda a: -a, mat_rows(low, j)), carry)
        put_mat(fw, carry, j)
        return carry

    last_f = lax.fori_loop(1, J, fw_step, first)
    steps = (1, 2, 4)
    whole = last_f
    for level, s in enumerate(steps):
        put_mat(scan_f, mat_map(lambda a: jnp.where(chunk >= s, a, 0.0), whole), level)
        moved = mat_mat(whole, mat_map(lambda a: pltpu.roll(a, s, 0), whole))
        whole = mat_map(lambda a, b: jnp.where(chunk >= s, b, a), whole, moved)
    send_map(0, whole, K - 1)
    before = mat_map(lambda a: pltpu.roll(a, 1, 0), whole)
    before = [[jnp.where(chunk >= 1, before[c][e], 1.0 if c == e else 0.0) for e in range(N)] for c in range(N)]
    put_mat(excl, before, 0)
    ld_upp.wait()
    start_b = mat_map(lambda a: -a, mat_rows(upp, J - 1))
    put_mat(bw, start_b, J - 1)
    put_mat(gw, last_f, J - 1)

    def bw_step(i, carry):
        j = J - 2 - i
        carry = mat_mat(mat_map(lambda a: -a, mat_rows(upp, j)), carry)
        put_mat(bw, carry, j)
        return carry

    def gw_step(i, carry):
        j = J - 2 - i
        moved = mat_mat(mat_rows(upp, j), carry)
        carry = mat_map(lambda a, b: a - b, get_mat(fw, j), moved)
        put_mat(gw, carry, j)
        return carry

    first_b = lax.fori_loop(0, J - 1, bw_step, start_b)
    first_g = lax.fori_loop(0, J - 1, gw_step, last_f)

    seen = mat_mat(first_g, before)
    put_mat(excl, seen, 1)

    whole = first_b
    for level, s in enumerate(steps):
        put_mat(scan_b, mat_map(lambda a: jnp.where(chunk < K - s, a, 0.0), whole), level)
        moved = mat_mat(whole, mat_map(lambda a: pltpu.roll(a, K - s, 0), whole))
        whole = mat_map(lambda a, b: jnp.where(chunk < K - s, b, a), whole, moved)
    send_map(1, whole, 0)
    after = mat_map(lambda a: pltpu.roll(a, K - 1, 0), whole)
    after = [[jnp.where(chunk < K - 1, after[c][e], 1.0 if c == e else 0.0) for e in range(N)] for c in range(N)]
    put_mat(excl, after, 2)
    seen = get_mat(excl, 1)
    for level, s in enumerate(steps):
        moved = mat_mat(get_mat(scan_b, level), mat_map(lambda a: pltpu.roll(a, K - s, 0), seen))
        seen = mat_map(jnp.add, seen, moved)
    send_map(2, seen, 0)
    put_mat(excl, mat_map(lambda a: jnp.where(chunk < K - 1, pltpu.roll(a, K - 1, 0), 0.0), seen), 1)

    for sweep in range(SWEEPS):
        if sweep == 0:
            ld_don.wait()
        places = [don[pl.ds(j, K, stride=J), :] for j in range(J)]
        row_of = [p >> 7 for p in places]
        col_of = [p & (LANES - 1) for p in places]

        def gather_step(jj, carry):
            carry = list(carry)
            for k in range(K):
                if sweep == 0:
                    ones = [xb[pl.ds((k * J + jj) * N + c, 1), :] for c in range(N)]
                else:
                    ones = [xk[sweep - 1, jj * N + c, k:k + 1, :] for c in range(N)]
                rows = [jnp.broadcast_to(one, (K, LANES)) for one in ones]
                for j in range(J):
                    hit = row_of[j] == k * J + jj
                    for c in range(N):
                        got = lane_gather(rows[c], col_of[j])
                        carry[j * N + c] = jnp.where(hit, got, carry[j * N + c])
            return carry

        got = lax.fori_loop(0, J, gather_step, [jnp.zeros((K, LANES), jnp.float32)] * (J * N))
        for i in range(J * N):
            donated[i] = got[i]

        if sweep == 0:
            for load in (ld_src, ld_ibl, ld_cpl):
                load.wait()
        for copy in edge_now:
            copy.wait_recv()
        left = edge_in[sweep, 0]
        right = edge_in[sweep, sides_stream - 1]
        lows, highs = [], []
        for j in range(J):
            rows = x_rows(sweep, j)
            flag = ibl[pl.ds(j, K, stride=J), :]
            lows, highs = [], []
            for c in range(N):
                i = j * N + c
                lows.append(jnp.where(lane == 0, pltpu.roll(left, (LANES - 2 * i) % LANES, 1), pltpu.roll(rows[c], 1, 1)))
                highs.append(jnp.where(lane == LANES - 1, pltpu.roll(right, LANES - 2 - 2 * i, 1), pltpu.roll(rows[c], LANES - 1, 1)))
            c2 = mat_rows(cpl, j, 2 * J * K * N * N)
            c3 = mat_rows(cpl, j, 3 * J * K * N * N)
            s_rows = vec_rows(src, j)
            for c in range(N):
                acc = s_rows[c] + jnp.where(flag == 2, donated[j * N + c], 0.0)
                for e in range(N):
                    acc = acc - (c2[e][c] * lows[e] + c3[e][c] * highs[e])
                base[j * N + c] = acc

        if sweep == 0:
            for copy in span_now:
                copy.wait_recv()
            ld_piv.wait()

        def forward_step(j, state):
            c0 = mat_rows(cpl, j)
            c1 = mat_rows(cpl, j, J * K * N * N)
            flag = ibl[pl.ds(j, K, stride=J), :]
            if sweep == 0:
                sides = [vec_rows(plane.at[i], j) for i in range(sides_span)]
            else:
                sides = [[plane_k[sweep - 1, i, j * N + c] for c in range(N)] for i in range(sides_span)]
            x0 = sides[0]
            rhs = []
            if sides_span == 1:
                both = mat_map(jnp.add, c0, c1)
                for c in range(N):
                    acc = functools.reduce(jnp.add, [both[e][c] * x0[e] for e in range(N)])
                    rhs.append(jnp.where(flag == 0, 0.0, base[j * N + c] - acc))
            else:
                x1 = sides[1]
                for c in range(N):
                    acc = functools.reduce(jnp.add, [c0[e][c] * x0[e] + c1[e][c] * x1[e] for e in range(N)])
                    rhs.append(jnp.where(flag == 0, 0.0, base[j * N + c] - acc))
            scaled = mat_vec(mat_rows(piv, j), rhs)
            moved = mat_vec(mat_rows(low, j), state)
            state = [a - b for a, b in zip(scaled, moved)]
            for c in range(N):
                work[j * N + c] = state[c]
            return state

        zero = [jnp.zeros((K, LANES), jnp.float32)] * N
        f = zero
        for j in range(J):
            if sweep > 0 and j % group == 0:
                for copy in piece_copies(sweep, j // group):
                    copy.wait_recv()
            f = forward_step(j, f)

        def backward_step(i, state):
            j = J - 1 - i
            moved = mat_vec(mat_rows(upp, j), state)
            state = [work[j * N + c] - moved[c] for c in range(N)]
            for c in range(N):
                work[j * N + c] = state[c]
            return state

        b = lax.fori_loop(0, J, backward_step, zero, unroll=True)
        for level, s in enumerate(steps):
            f = vec_add(f, mat_vec(get_mat(scan_f, level), [pltpu.roll(v, s, 0) for v in f]))
        y_in = [jnp.where(chunk >= 1, pltpu.roll(v, 1, 0), 0.0) for v in f]
        b = vec_add(b, mat_vec(get_mat(gw, 0), y_in))
        for level, s in enumerate(steps):
            b = vec_add(b, mat_vec(get_mat(scan_b, level), [pltpu.roll(v, K - s, 0) for v in b]))
        x_in = [jnp.where(chunk < K - 1, pltpu.roll(v, K - 1, 0), 0.0) for v in b]
        for c in range(N):
            vec_all[sweep, me, pl.ds(c, 1), :] = f[c][K - 1:K]
            vec_all[sweep, me, pl.ds(K + c, 1), :] = b[c][0:1]
        sends = normal_copies(vec_all.at[sweep], vec_send.at[sweep], vec_recv.at[sweep])
        for copy in sends:
            copy.start()
        pending += sends
        if sweep == 0:
            for part in range(3):
                for used, copy in map_copies(part, True):
                    @pl.when(used)
                    def _(copy=copy):
                        copy.wait_recv()
        for copy in normal_arrivals(vec_all.at[sweep], vec_send.at[sweep], vec_recv.at[sweep]):
            copy.wait_recv()

        def apply_map(d, m, state):
            return functools.reduce(jnp.add, [
                map_all[m, d, pl.ds(e, N, stride=N), :] * state[e:e + 1] for e in range(N)])

        none = jnp.zeros((N, LANES), jnp.float32)
        entries, state, mine = [none], none, none
        for d in range(n_normal - 1):
            state = vec_all[sweep, d, pl.ds(0, N), :] + apply_map(d, 0, state)
            entries.append(state)
            mine = jnp.where(me == d + 1, state, mine)
        x_state, x_mine = none, none
        for d in range(n_normal - 1, 0, -1):
            x_state = (vec_all[sweep, d, pl.ds(K, N), :] + apply_map(d, 2, entries[d])) + apply_map(d, 1, x_state)
            x_mine = jnp.where(me == d - 1, x_state, x_mine)
        y_entry = [jnp.broadcast_to(mine[c:c + 1], (K, LANES)) for c in range(N)]
        x_entry = [jnp.broadcast_to(x_mine[c:c + 1], (K, LANES)) for c in range(N)]
        y_in = vec_add(y_in, mat_vec(get_mat(excl, 0), y_entry))
        x_in = vec_add(x_in, mat_vec(get_mat(excl, 1), y_entry))
        x_in = vec_add(x_in, mat_vec(get_mat(excl, 2), x_entry))

        for j in range(J):
            more = vec_add(mat_vec(get_mat(gw, j), y_in), mat_vec(get_mat(bw, j), x_in))
            for c in range(N):
                value = work[j * N + c] + more[c]
                if sweep == SWEEPS - 1:
                    out_ref[pl.ds(j * N + c, K, stride=J * N), :] = value
                else:
                    xk[sweep, j * N + c] = value
            if sweep < SWEEPS - 1 and j % group == group - 1:
                copies = piece_copies(sweep + 1, j // group)
                for copy in copies:
                    copy.start()
                pending += copies
        if sweep < SWEEPS - 1:
            edge_now = send_edges(sweep + 1)
            pending += edge_now

    for copy in pending:
        copy.wait_send()
    for part in range(3):
        for used, copy in map_copies(part, False):
            @pl.when(used)
            def _(copy=copy):
                copy.wait_send()


def per_device(sizes, iterate, source, pivot, lower, upper, coupling, iblank, donor):
    points, comps, planes, lines = iterate.shape
    n_normal, n_span, n_stream = sizes
    J = points // K
    rows, mats = points * N, points * N * N
    sides_span, sides_stream = (1 if n_span == 2 else 2), (1 if n_stream == 2 else 2)
    f32 = jnp.float32
    peers = max(n_normal - 1, 1)
    scratch = [
        pltpu.VMEM((rows, LANES), f32),
        pltpu.VMEM((SWEEPS - 1, J * N, K, LANES), f32),
        pltpu.VMEM((rows, LANES), f32),
        pltpu.VMEM((mats, LANES), f32),
        pltpu.VMEM((mats, LANES), f32),
        pltpu.VMEM((mats, LANES), f32),
        pltpu.VMEM((4 * mats, LANES), f32),
        pltpu.VMEM((points, LANES), jnp.int32),
        pltpu.VMEM((points, LANES), jnp.int32),
        pltpu.VMEM((sides_span, rows, LANES), f32),
        pltpu.VMEM((SWEEPS - 1, sides_span, J * N, K, LANES), f32),
        pltpu.VMEM((SWEEPS, K, LANES), f32),
        pltpu.VMEM((SWEEPS, sides_stream, K, LANES), f32),
        pltpu.VMEM((SWEEPS, n_normal, 2 * K, LANES), f32),
        pltpu.VMEM((3, n_normal, N * N, LANES), f32),
        pltpu.VMEM((J, N, N, K, LANES), f32),
        pltpu.VMEM((J, N, N, K, LANES), f32),
        pltpu.VMEM((J, N, N, K, LANES), f32),
        pltpu.VMEM((3, N, N, K, LANES), f32),
        pltpu.VMEM((3, N, N, K, LANES), f32),
        pltpu.VMEM((3, N, N, K, LANES), f32),
        pltpu.VMEM((J * N, K, LANES), f32),
        pltpu.VMEM((J * N, K, LANES), f32),
        pltpu.VMEM((J * N, K, LANES), f32),
        pltpu.SemaphoreType.DMA((8,)),
        pltpu.SemaphoreType.DMA((sides_span,)),
        pltpu.SemaphoreType.DMA((sides_span,)),
        pltpu.SemaphoreType.DMA((SWEEPS - 1, J, sides_span)),
        pltpu.SemaphoreType.DMA((SWEEPS - 1, J, sides_span)),
        pltpu.SemaphoreType.DMA((SWEEPS, sides_stream)),
        pltpu.SemaphoreType.DMA((SWEEPS, sides_stream)),
        pltpu.SemaphoreType.DMA((SWEEPS, peers)),
        pltpu.SemaphoreType.DMA((SWEEPS, peers)),
        pltpu.SemaphoreType.DMA((3, peers)),
        pltpu.SemaphoreType.DMA((3, peers)),
    ]
    out = pl.pallas_call(
        functools.partial(kernel, sizes, J),
        out_shape=pltpu.VMEM((rows, LANES), f32),
        in_specs=[pl.BlockSpec(memory_space=pltpu.HBM)] * 8,
        out_specs=pl.BlockSpec(memory_space=pltpu.VMEM),
        scratch_shapes=scratch,
        compiler_params=pltpu.CompilerParams(
            collective_id=0, has_side_effects=True, vmem_limit_bytes=32 * 1024 * 1024),
        cost_estimate=pl.CostEstimate(flops=12000000, bytes_accessed=5000000, transcendentals=0),
    )(*[
        pltpu.with_memory_space_constraint(operand, pltpu.HBM) for operand in (
            iterate.reshape(rows, lines), source.reshape(rows, lines), pivot.reshape(mats, lines),
            lower.reshape(mats, lines), upper.reshape(mats, lines), coupling.reshape(4 * mats, lines),
            iblank.reshape(points, lines), donor.reshape(points, lines))
    ])
    return out.reshape(points, comps, planes, lines)


def solution(mesh):
    placed = (
        P("normal", None, "span", "stream"),
        P("normal", None, "span", "stream"),
        P("normal", None, None, "span", "stream"),
        P("normal", None, None, "span", "stream"),
        P("normal", None, None, "span", "stream"),
        P(None, "normal", None, None, "span", "stream"),
        P("normal", "span", "stream"),
        P("normal", "span", "stream"),
    )
    sizes = tuple(mesh.shape[name] for name in ("normal", "span", "stream"))
    return jax.shard_map(
        functools.partial(per_device, sizes),
        mesh=mesh,
        in_specs=placed,
        out_specs=P("normal", None, "span", "stream"),
        check_vma=False,
    )
```

```python
import functools
import jax
import jax.numpy as jnp
from jax import lax
from jax.experimental import pallas as pl
from jax.experimental.pallas import tpu as pltpu
from jax.sharding import PartitionSpec as P

SWEEPS = 2
N = 5
K = 8
LANES = 128
MESH = pl.DeviceIdType.MESH


def tree_sum(terms):
    while len(terms) > 1:
        terms = [a + b for a, b in zip(terms[::2], terms[1::2])] + ([terms[-1]] if len(terms) % 2 else [])
    return terms[0]


def mat_vec(mat, vec):
    return [tree_sum([mat[c][e] * vec[e] for e in range(N)]) for c in range(N)]


def mat_mat(left_row, right, finish):
    out = []
    for c in range(N):
        row = left_row(c)
        sums = []
        for f in range(N):
            total = row[0] * right[0][f]
            for e in range(1, N):
                total = total + row[e] * right[e][f]
            sums.append(total)
        out.append(finish(c, sums))
    return out


def mat_map(function, *mats):
    return [[function(*(m[c][e] for m in mats)) for e in range(N)] for c in range(N)]


def vec_add(a, b):
    return [p + q for p, q in zip(a, b)]


def lane_gather(row, index):
    numbers = lax.GatherDimensionNumbers(
        offset_dims=(), collapsed_slice_dims=(1,), start_index_map=(1,),
        operand_batching_dims=(0,), start_indices_batching_dims=(0,))
    return lax.gather(row, index[..., None], numbers, (1, 1), mode=lax.GatherScatterMode.PROMISE_IN_BOUNDS)


def kernel(sizes, per_chunk, x_hbm, src_hbm, piv_hbm, low_hbm, upp_hbm, cpl_hbm, ibl_hbm, don_hbm, out_ref,
           xb, xk, src, piv, low, upp, cpl, ibl, don, plane, plane_k, edge_out, edge_in, vec_all, map_all,
           fw, gw, bw, scan_f, scan_b, excl, base, work, donated,
           load_sem, span_send, span_recv, piece_send, piece_recv, edge_send, edge_recv, vec_send, vec_recv, map_send, map_recv):
    J = per_chunk
    n_normal, n_span, n_stream = sizes
    me, sp, st = lax.axis_index("normal"), lax.axis_index("span"), lax.axis_index("stream")
    span_targets = [lax.rem(sp + 1, n_span)] if n_span == 2 else [lax.rem(sp + 1, n_span), lax.rem(sp + n_span - 1, n_span)]
    stream_targets = [lax.rem(st + 1, n_stream)] if n_stream == 2 else [lax.rem(st + 1, n_stream), lax.rem(st + n_stream - 1, n_stream)]
    sides_span, sides_stream = len(span_targets), len(stream_targets)

    pairs = [(x_hbm, xb), (low_hbm, low), (upp_hbm, upp), (don_hbm, don), (cpl_hbm, cpl),
             (src_hbm, src), (ibl_hbm, ibl), (piv_hbm, piv)]
    loads = [pltpu.make_async_copy(a, b, load_sem.at[i]) for i, (a, b) in enumerate(pairs)]
    for load in loads:
        load.start()
    ld_x, ld_low, ld_upp, ld_don, ld_cpl, ld_src, ld_ibl, ld_piv = loads

    barrier = pltpu.get_barrier_semaphore()
    for t in span_targets:
        pl.semaphore_signal(barrier, inc=1, device_id={"span": t}, device_id_type=MESH)
    for t in stream_targets:
        pl.semaphore_signal(barrier, inc=1, device_id={"stream": t}, device_id_type=MESH)
    for o in range(1, n_normal):
        pl.semaphore_signal(barrier, inc=1, device_id={"normal": lax.rem(me + o, n_normal)}, device_id_type=MESH)
    pl.semaphore_wait(barrier, sides_span + sides_stream + n_normal - 1)

    def span_copies():
        return [
            pltpu.make_async_remote_copy(
                src_ref=x_hbm, dst_ref=plane.at[i], send_sem=span_send.at[i],
                recv_sem=span_recv.at[i], device_id={"span": t}, device_id_type=MESH)
            for i, t in enumerate(span_targets)
        ]

    group = 2 if J % 2 == 0 else 1

    def piece_copies(sweep, piece):
        part = pl.ds(piece * group * N, group * N)
        return [
            pltpu.make_async_remote_copy(
                src_ref=xk.at[sweep - 1, part], dst_ref=plane_k.at[sweep - 1, i, part],
                send_sem=piece_send.at[sweep - 1, piece, i], recv_sem=piece_recv.at[sweep - 1, piece, i],
                device_id={"span": t}, device_id_type=MESH)
            for i, t in enumerate(span_targets)
        ]

    def edge_copies(sweep):
        return [
            pltpu.make_async_remote_copy(
                src_ref=edge_out.at[sweep], dst_ref=edge_in.at[sweep, i], send_sem=edge_send.at[sweep, i],
                recv_sem=edge_recv.at[sweep, i], device_id={"stream": t}, device_id_type=MESH)
            for i, t in enumerate(stream_targets)
        ]

    def normal_copies(ref, sends, recvs):
        out = []
        for o in range(1, n_normal):
            out.append(pltpu.make_async_remote_copy(
                src_ref=ref.at[me], dst_ref=ref.at[me], send_sem=sends.at[o - 1], recv_sem=recvs.at[o - 1],
                device_id={"normal": lax.rem(me + o, n_normal)}, device_id_type=MESH))
        return out

    def normal_arrivals(ref, sends, recvs):
        out = []
        for o in range(1, n_normal):
            came = lax.rem(me + n_normal - o, n_normal)
            out.append(pltpu.make_async_remote_copy(
                src_ref=ref.at[me], dst_ref=ref.at[came], send_sem=sends.at[o - 1], recv_sem=recvs.at[o - 1],
                device_id={"normal": lax.rem(me + o, n_normal)}, device_id_type=MESH))
        return out

    def map_copies(part, arriving):
        out = []
        for o in range(1, n_normal):
            slot = lax.rem(me + n_normal - o, n_normal) if arriving else me
            copy = pltpu.make_async_remote_copy(
                src_ref=map_all.at[part, me], dst_ref=map_all.at[part, slot],
                send_sem=map_send.at[part, o - 1], recv_sem=map_recv.at[part, o - 1],
                device_id={"normal": lax.rem(me + o, n_normal)}, device_id_type=MESH)
            if part == 0:
                used = slot < n_normal - 1
            else:
                used = me - o < 0 if arriving else me + o >= n_normal
            out.append((used, copy))
        return out

    def send_map(part, mat, row):
        for c in range(N):
            for e in range(N):
                map_all[part, me, pl.ds(c * N + e, 1), :] = mat[c][e][row:row + 1]
        for used, copy in map_copies(part, False):
            @pl.when(used)
            def _(copy=copy):
                copy.start()

    lane = lax.broadcasted_iota(jnp.int32, (K, LANES), 1)
    chunk = lax.broadcasted_iota(jnp.int32, (K, LANES), 0)

    def vec_rows(ref, j):
        return [ref[pl.ds(j * N + c, K, stride=J * N), :] for c in range(N)]

    def mat_rows(ref, j, first=0):
        return [[ref[pl.ds(first + j * N * N + c * N + e, K, stride=J * N * N), :] for e in range(N)] for c in range(N)]

    def block_row(ref, j):
        return lambda c: [ref[pl.ds(j * N * N + c * N + e, K, stride=J * N * N), :] for e in range(N)]

    def kept_row(ref, *at):
        return lambda c: [ref[(*at, c, e)] for e in range(N)]

    def keep(ref, *at, sign=1):
        def finish(c, sums):
            sums = [-v for v in sums] if sign < 0 else sums
            for e in range(N):
                ref[(*at, c, e)] = sums[e]
            return sums
        return finish

    def double(scan, level, whole, shift, mask):
        put_mat(scan, mat_map(lambda a: jnp.where(mask, a, 0.0), whole), level)
        rolled = mat_map(lambda a: pltpu.roll(a, shift, 0), whole)
        return mat_mat(kept_row(scan, level), rolled,
                       lambda c, sums: [jnp.where(mask, b, a) for a, b in zip(whole[c], sums)])

    def get_mat(ref, *at):
        return [[ref[(*at, c, e)] for e in range(N)] for c in range(N)]

    def put_mat(ref, mat, *at):
        for c in range(N):
            for e in range(N):
                ref[(*at, c, e)] = mat[c][e]

    def x_rows(sweep, j):
        if sweep == 0:
            return vec_rows(xb, j)
        return [xk[sweep - 1, j * N + c] for c in range(N)]

    def send_edges(sweep):
        packed = jnp.zeros((K, LANES), jnp.float32)
        for j in range(J):
            rows = x_rows(sweep, j)
            for c in range(N):
                i = j * N + c
                packed = jnp.where(lane >> 1 == i, pltpu.roll(rows[c], 2 * i + 1, 1), packed)
        edge_out[sweep] = packed
        copies = edge_copies(sweep)
        for copy in copies:
            copy.start()
        return copies

    span_now = span_copies()
    for copy in span_now:
        copy.start()
    ld_x.wait()
    edge_now = send_edges(0)
    pending = list(span_now) + list(edge_now)

    for part in (1, 2):
        for d in range(n_normal - 1):
            @pl.when(d < me)
            def _(part=part, d=d):
                map_all[part, d] = jnp.zeros((N * N, LANES), jnp.float32)

    ld_low.wait()

    first = mat_map(lambda a: -a, mat_rows(low, 0))
    put_mat(fw, first, 0)

    def fw_step(j, carry):
        return mat_mat(block_row(low, j), carry, keep(fw, j, sign=-1))

    last_f = lax.fori_loop(1, J, fw_step, first)
    steps = (1, 2, 4)
    whole = last_f
    for level, s in enumerate(steps):
        whole = double(scan_f, level, whole, s, chunk >= s)
    send_map(0, whole, K - 1)
    before = mat_map(lambda a: pltpu.roll(a, 1, 0), whole)
    before = [[jnp.where(chunk >= 1, before[c][e], 1.0 if c == e else 0.0) for e in range(N)] for c in range(N)]
    put_mat(excl, before, 0)
    ld_upp.wait()
    start_b = mat_map(lambda a: -a, mat_rows(upp, J - 1))
    put_mat(bw, start_b, J - 1)
    put_mat(gw, last_f, J - 1)

    def bw_step(i, carry):
        j = J - 2 - i
        return mat_mat(block_row(upp, j), carry, keep(bw, j, sign=-1))

    def gw_step(i, carry):
        j = J - 2 - i

        def finish(c, sums):
            return keep(gw, j)(c, [fw[j, c, e] - sums[e] for e in range(N)])

        return mat_mat(block_row(upp, j), carry, finish)

    first_b = lax.fori_loop(0, J - 1, bw_step, start_b)
    lax.fori_loop(0, J - 1, gw_step, last_f)

    mat_mat(kept_row(gw, 0), get_mat(excl, 0), keep(excl, 1))

    whole = first_b
    for level, s in enumerate(steps):
        whole = double(scan_b, level, whole, K - s, chunk < K - s)
    send_map(1, whole, 0)
    after = mat_map(lambda a: pltpu.roll(a, K - 1, 0), whole)
    after = [[jnp.where(chunk < K - 1, after[c][e], 1.0 if c == e else 0.0) for e in range(N)] for c in range(N)]
    put_mat(excl, after, 2)
    seen = get_mat(excl, 1)
    for level, s in enumerate(steps):
        rolled = mat_map(lambda a: pltpu.roll(a, K - s, 0), seen)
        seen = mat_mat(kept_row(scan_b, level), rolled,
                       lambda c, sums, seen=seen: vec_add(seen[c], sums))
    send_map(2, seen, 0)
    put_mat(excl, mat_map(lambda a: jnp.where(chunk < K - 1, pltpu.roll(a, K - 1, 0), 0.0), seen), 1)

    for sweep in range(SWEEPS):
        if sweep == 0:
            ld_don.wait()
        places = [don[pl.ds(j, K, stride=J), :] for j in range(J)]
        row_of = [p >> 7 for p in places]
        col_of = [p & (LANES - 1) for p in places]

        def gather_step(jj, carry):
            carry = list(carry)
            for k in range(K):
                if sweep == 0:
                    ones = [xb[pl.ds((k * J + jj) * N + c, 1), :] for c in range(N)]
                else:
                    ones = [xk[sweep - 1, jj * N + c, k:k + 1, :] for c in range(N)]
                rows = [jnp.broadcast_to(one, (K, LANES)) for one in ones]
                for j in range(J):
                    hit = row_of[j] == k * J + jj
                    for c in range(N):
                        got = lane_gather(rows[c], col_of[j])
                        carry[j * N + c] = jnp.where(hit, got, carry[j * N + c])
            return carry

        got = lax.fori_loop(0, J, gather_step, [jnp.zeros((K, LANES), jnp.float32)] * (J * N))
        for i in range(J * N):
            donated[i] = got[i]

        if sweep == 0:
            for load in (ld_src, ld_ibl, ld_cpl):
                load.wait()
        for copy in edge_now:
            copy.wait_recv()
        left = edge_in[sweep, 0]
        right = edge_in[sweep, sides_stream - 1]
        lows, highs = [], []
        for j in range(J):
            rows = x_rows(sweep, j)
            flag = ibl[pl.ds(j, K, stride=J), :]
            lows, highs = [], []
            for c in range(N):
                i = j * N + c
                lows.append(jnp.where(lane == 0, pltpu.roll(left, (LANES - 2 * i) % LANES, 1), pltpu.roll(rows[c], 1, 1)))
                highs.append(jnp.where(lane == LANES - 1, pltpu.roll(right, LANES - 2 - 2 * i, 1), pltpu.roll(rows[c], LANES - 1, 1)))
            c2 = mat_rows(cpl, j, 2 * J * K * N * N)
            c3 = mat_rows(cpl, j, 3 * J * K * N * N)
            s_rows = vec_rows(src, j)
            for c in range(N):
                acc = s_rows[c] + jnp.where(flag == 2, donated[j * N + c], 0.0)
                for e in range(N):
                    acc = acc - (c2[e][c] * lows[e] + c3[e][c] * highs[e])
                base[j * N + c] = acc

        if sweep == 0:
            for copy in span_now:
                copy.wait_recv()
            ld_piv.wait()

        def forward_step(j, state):
            c0 = mat_rows(cpl, j)
            c1 = mat_rows(cpl, j, J * K * N * N)
            flag = ibl[pl.ds(j, K, stride=J), :]
            if sweep == 0:
                sides = [vec_rows(plane.at[i], j) for i in range(sides_span)]
            else:
                sides = [[plane_k[sweep - 1, i, j * N + c] for c in range(N)] for i in range(sides_span)]
            x0 = sides[0]
            rhs = []
            if sides_span == 1:
                both = mat_map(jnp.add, c0, c1)
                for c in range(N):
                    acc = functools.reduce(jnp.add, [both[e][c] * x0[e] for e in range(N)])
                    rhs.append(jnp.where(flag == 0, 0.0, base[j * N + c] - acc))
            else:
                x1 = sides[1]
                for c in range(N):
                    acc = functools.reduce(jnp.add, [c0[e][c] * x0[e] + c1[e][c] * x1[e] for e in range(N)])
                    rhs.append(jnp.where(flag == 0, 0.0, base[j * N + c] - acc))
            scaled = mat_vec(mat_rows(piv, j), rhs)
            moved = mat_vec(mat_rows(low, j), state)
            state = [a - b for a, b in zip(scaled, moved)]
            for c in range(N):
                work[j * N + c] = state[c]
            return state

        zero = [jnp.zeros((K, LANES), jnp.float32)] * N
        f = zero
        for j in range(J):
            if sweep > 0 and j % group == 0:
                for copy in piece_copies(sweep, j // group):
                    copy.wait_recv()
            f = forward_step(j, f)

        def backward_step(i, state):
            j = J - 1 - i
            moved = mat_vec(mat_rows(upp, j), state)
            state = [work[j * N + c] - moved[c] for c in range(N)]
            for c in range(N):
                work[j * N + c] = state[c]
            return state

        b = lax.fori_loop(0, J, backward_step, zero, unroll=True)
        for level, s in enumerate(steps):
            f = vec_add(f, mat_vec(get_mat(scan_f, level), [pltpu.roll(v, s, 0) for v in f]))
        y_in = [jnp.where(chunk >= 1, pltpu.roll(v, 1, 0), 0.0) for v in f]
        b = vec_add(b, mat_vec(get_mat(gw, 0), y_in))
        for level, s in enumerate(steps):
            b = vec_add(b, mat_vec(get_mat(scan_b, level), [pltpu.roll(v, K - s, 0) for v in b]))
        x_in = [jnp.where(chunk < K - 1, pltpu.roll(v, K - 1, 0), 0.0) for v in b]
        for c in range(N):
            vec_all[sweep, me, pl.ds(c, 1), :] = f[c][K - 1:K]
            vec_all[sweep, me, pl.ds(K + c, 1), :] = b[c][0:1]
        sends = normal_copies(vec_all.at[sweep], vec_send.at[sweep], vec_recv.at[sweep])
        for copy in sends:
            copy.start()
        pending += sends
        if sweep == 0:
            for part in range(3):
                for used, copy in map_copies(part, True):
                    @pl.when(used)
                    def _(copy=copy):
                        copy.wait_recv()
        for copy in normal_arrivals(vec_all.at[sweep], vec_send.at[sweep], vec_recv.at[sweep]):
            copy.wait_recv()

        def apply_map(d, m, state):
            return functools.reduce(jnp.add, [
                map_all[m, d, pl.ds(e, N, stride=N), :] * state[e:e + 1] for e in range(N)])

        none = jnp.zeros((N, LANES), jnp.float32)
        entries, state, mine = [none], none, none
        for d in range(n_normal - 1):
            state = vec_all[sweep, d, pl.ds(0, N), :] + apply_map(d, 0, state)
            entries.append(state)
            mine = jnp.where(me == d + 1, state, mine)
        x_state, x_mine = none, none
        for d in range(n_normal - 1, 0, -1):
            x_state = (vec_all[sweep, d, pl.ds(K, N), :] + apply_map(d, 2, entries[d])) + apply_map(d, 1, x_state)
            x_mine = jnp.where(me == d - 1, x_state, x_mine)
        y_entry = [jnp.broadcast_to(mine[c:c + 1], (K, LANES)) for c in range(N)]
        x_entry = [jnp.broadcast_to(x_mine[c:c + 1], (K, LANES)) for c in range(N)]
        y_in = vec_add(y_in, mat_vec(get_mat(excl, 0), y_entry))
        x_in = vec_add(x_in, mat_vec(get_mat(excl, 1), y_entry))
        x_in = vec_add(x_in, mat_vec(get_mat(excl, 2), x_entry))

        for j in range(J):
            more = vec_add(mat_vec(get_mat(gw, j), y_in), mat_vec(get_mat(bw, j), x_in))
            for c in range(N):
                value = work[j * N + c] + more[c]
                if sweep == SWEEPS - 1:
                    out_ref[pl.ds(j * N + c, K, stride=J * N), :] = value
                else:
                    xk[sweep, j * N + c] = value
            if sweep < SWEEPS - 1 and j % group == group - 1:
                copies = piece_copies(sweep + 1, j // group)
                for copy in copies:
                    copy.start()
                pending += copies
        if sweep < SWEEPS - 1:
            edge_now = send_edges(sweep + 1)
            pending += edge_now

    for copy in pending:
        copy.wait_send()
    for part in range(3):
        for used, copy in map_copies(part, False):
            @pl.when(used)
            def _(copy=copy):
                copy.wait_send()


def per_device(sizes, iterate, source, pivot, lower, upper, coupling, iblank, donor):
    points, comps, planes, lines = iterate.shape
    n_normal, n_span, n_stream = sizes
    J = points // K
    rows, mats = points * N, points * N * N
    sides_span, sides_stream = (1 if n_span == 2 else 2), (1 if n_stream == 2 else 2)
    f32 = jnp.float32
    peers = max(n_normal - 1, 1)
    scratch = [
        pltpu.VMEM((rows, LANES), f32),
        pltpu.VMEM((SWEEPS - 1, J * N, K, LANES), f32),
        pltpu.VMEM((rows, LANES), f32),
        pltpu.VMEM((mats, LANES), f32),
        pltpu.VMEM((mats, LANES), f32),
        pltpu.VMEM((mats, LANES), f32),
        pltpu.VMEM((4 * mats, LANES), f32),
        pltpu.VMEM((points, LANES), jnp.int32),
        pltpu.VMEM((points, LANES), jnp.int32),
        pltpu.VMEM((sides_span, rows, LANES), f32),
        pltpu.VMEM((SWEEPS - 1, sides_span, J * N, K, LANES), f32),
        pltpu.VMEM((SWEEPS, K, LANES), f32),
        pltpu.VMEM((SWEEPS, sides_stream, K, LANES), f32),
        pltpu.VMEM((SWEEPS, n_normal, 2 * K, LANES), f32),
        pltpu.VMEM((3, n_normal, N * N, LANES), f32),
        pltpu.VMEM((J, N, N, K, LANES), f32),
        pltpu.VMEM((J, N, N, K, LANES), f32),
        pltpu.VMEM((J, N, N, K, LANES), f32),
        pltpu.VMEM((3, N, N, K, LANES), f32),
        pltpu.VMEM((3, N, N, K, LANES), f32),
        pltpu.VMEM((3, N, N, K, LANES), f32),
        pltpu.VMEM((J * N, K, LANES), f32),
        pltpu.VMEM((J * N, K, LANES), f32),
        pltpu.VMEM((J * N, K, LANES), f32),
        pltpu.SemaphoreType.DMA((8,)),
        pltpu.SemaphoreType.DMA((sides_span,)),
        pltpu.SemaphoreType.DMA((sides_span,)),
        pltpu.SemaphoreType.DMA((SWEEPS - 1, J, sides_span)),
        pltpu.SemaphoreType.DMA((SWEEPS - 1, J, sides_span)),
        pltpu.SemaphoreType.DMA((SWEEPS, sides_stream)),
        pltpu.SemaphoreType.DMA((SWEEPS, sides_stream)),
        pltpu.SemaphoreType.DMA((SWEEPS, peers)),
        pltpu.SemaphoreType.DMA((SWEEPS, peers)),
        pltpu.SemaphoreType.DMA((3, peers)),
        pltpu.SemaphoreType.DMA((3, peers)),
    ]
    out = pl.pallas_call(
        functools.partial(kernel, sizes, J),
        out_shape=pltpu.VMEM((rows, LANES), f32),
        in_specs=[pl.BlockSpec(memory_space=pltpu.HBM)] * 8,
        out_specs=pl.BlockSpec(memory_space=pltpu.VMEM),
        scratch_shapes=scratch,
        compiler_params=pltpu.CompilerParams(
            collective_id=0, has_side_effects=True, vmem_limit_bytes=32 * 1024 * 1024),
        cost_estimate=pl.CostEstimate(flops=12000000, bytes_accessed=5000000, transcendentals=0),
    )(*[
        pltpu.with_memory_space_constraint(operand, pltpu.HBM) for operand in (
            iterate.reshape(rows, lines), source.reshape(rows, lines), pivot.reshape(mats, lines),
            lower.reshape(mats, lines), upper.reshape(mats, lines), coupling.reshape(4 * mats, lines),
            iblank.reshape(points, lines), donor.reshape(points, lines))
    ])
    return out.reshape(points, comps, planes, lines)


def solution(mesh):
    placed = (
        P("normal", None, "span", "stream"),
        P("normal", None, "span", "stream"),
        P("normal", None, None, "span", "stream"),
        P("normal", None, None, "span", "stream"),
        P("normal", None, None, "span", "stream"),
        P(None, "normal", None, None, "span", "stream"),
        P("normal", "span", "stream"),
        P("normal", "span", "stream"),
    )
    sizes = tuple(mesh.shape[name] for name in ("normal", "span", "stream"))
    return jax.shard_map(
        functools.partial(per_device, sizes),
        mesh=mesh,
        in_specs=placed,
        out_specs=P("normal", None, "span", "stream"),
        check_vma=False,
    )
```
